128 devices in a mesh: gx: 8 (over z, core), gy: 16 (over x, y).
Axes of the slice: x: 4, y: 4, z: 4, core: 2. Of those that a mesh axis runs over, the one named last changes fastest.
Arguments:
- displacement: float32 [3, 256, 5, 2048], P(None, 'gx', None, 'gy'), may hold values from -5 to 5
- velocity: float32 [3, 256, 5, 2048], P(None, 'gx', None, 'gy'), may hold values from -4 to 4
- stiffness: float32 [256, 5, 2048], P('gx', None, 'gy'), may hold values from 0.5 to 2
- inverse_mass: float32 [256, 5, 2048], P('gx', None, 'gy'), may hold values from 0.5 to 2
- facing: int32 [256, 16, 8], P('gx', 'gy'), may hold values from 0 to 4095, as said below
Outputs:
- final_displacement: float32 [3, 256, 5, 2048], P(None, 'gx', None, 'gy')
- final_velocity: float32 [3, 256, 5, 2048], P(None, 'gx', None, 'gy')
The draws below stay inside these ranges and needn't reach their ends.
Inputs may be any that keep to these rules, and one draw needn't show every extreme that they name: facing[x, j, k] names block x' * 16 + j'. For each aligned run of 32 rows x and each j, the 256 entries name blocks with each pair (x' // 32, j') exactly 2 times; repeats are allowed.
All inputs are finite; a program needn't handle non-finite values.
Results may differ from the reference program's by a relative error of at most 0.0001.
Values sent between devices are 32-bit elements; how exact they have to be, the bound alone decides.
No kernel may reach another device: no remote copies, remote signals or barrier semaphores. Data moves between devices by JAX's collectives and lax.ppermute only.
A program may use at most 64 MiB of HBM per device.

```python
import math
import jax
import jax.numpy as jnp
from jax import lax

CX = 32
CY = 128
NZ = 5
STEPS = 2
NX = 256
NY = 2048
GROUPS = 16
CAP = 2
DEVICES = 128


def draw_facing(key, part):
    requests = 8 * CX
    seed_list = jax.random.split(key, DEVICES)
    order_list = jax.vmap(lambda seed_one: jax.random.permutation(seed_one, requests))(seed_list)
    target_device = order_list // CAP
    target_row = jax.random.randint(jax.random.fold_in(key, 7), (DEVICES, requests), 0, CX)
    target_row = jnp.where(order_list == 0, 0, target_row)
    target_row = jnp.where(order_list == requests - 1, CX - 1, target_row)
    target_x = target_device // GROUPS * CX + target_row
    numbers = target_x * GROUPS + target_device % GROUPS
    shaped = numbers.reshape(DEVICES // GROUPS, GROUPS, CX, 8).transpose(0, 2, 1, 3)
    return shaped.reshape(NX, GROUPS, 8).astype(jnp.int32)


def block_levels(key, shape, cuts, low, largest):
    def one(axis_at, parts):
        steps = jax.random.uniform(jax.random.fold_in(jax.random.fold_in(key, 6), axis_at), (parts,), jnp.float32, low / len(cuts), largest / len(cuts))
        return jnp.repeat(jnp.exp(steps), shape[axis_at] // parts).reshape((-1,) + (1,) * (len(shape) - axis_at - 1))

    level = one(*cuts[0])
    for cut in cuts[1:]:
        level = level * one(*cut)
    return level


def scatter_about(key, extent, scale, limit, pieces=(), kind=jnp.bfloat16):
    factor_of = block_levels(key, extent, pieces, -0.22, 0.18) if pieces else 1.0
    drawn = jax.random.normal(key, extent, jnp.float32) * scale * factor_of
    return jnp.minimum(jnp.maximum(drawn, -limit), limit).astype(kind)


def setup_inputs(seed: int = 0) -> dict:
    key_of = jax.random.split(jax.random.key(seed), 6)
    displacement = scatter_about(key_of[0], (3, NX, NZ, NY), 1.0, 5.0, ((1, 8), (3, 16)), jnp.float32)
    velocity = scatter_about(key_of[1], (3, NX, NZ, NY), 0.5, 4.0, ((1, 8), (3, 16)), jnp.float32)
    stiffness = jnp.clip(jnp.exp(math.log(2.0) - 1.3862944 * jax.random.uniform(key_of[2], (NX, NZ, NY), jnp.float32) ** block_levels(key_of[2], (NX, NZ, NY), ((0, 8), (2, 16)), -0.2, 0.2)), 0.5, 2.0)
    inverse_mass = jnp.clip(jnp.exp(math.log(2.0) - 1.3862944 * jax.random.uniform(key_of[3], (NX, NZ, NY), jnp.float32) ** block_levels(key_of[3], (NX, NZ, NY), ((0, 8), (2, 16)), -0.2, 0.2)), 0.5, 2.0)
    facing = draw_facing(jax.random.fold_in(key_of[5], 71), 0)
    return dict(displacement=displacement, velocity=velocity, stiffness=stiffness, inverse_mass=inverse_mass, facing=facing)


time_step = 0.2
penalty = 4.0
damping = 1.0
kernel_width = 4.0
frame_extent = 4.0


def block_frame(block_size):
    place = (jnp.arange(block_size, dtype=jnp.float32) - (block_size - 1) / 2.0) * (frame_extent / block_size)
    zero_row = jnp.zeros((block_size,), jnp.float32)
    return jnp.stack([zero_row, place, zero_row], axis=0)


def pair_forces(own_block, facing_blocks):
    block_size = own_block.shape[-1]
    frame = block_frame(block_size)
    own_disp = own_block[:, :3] + frame
    own_vel = own_block[:, 3:]
    far_disp = facing_blocks[:, :, :3] + frame
    far_vel = facing_blocks[:, :, 3:]
    gaps = own_disp[:, None, :, :, None] - far_disp[:, :, :, None, :]
    spread = jnp.sum(gaps * gaps, axis=2)
    weights = jnp.exp(-spread / kernel_width)
    row_total = jnp.sum(weights, axis=3)
    col_total = jnp.sum(weights, axis=2)
    highest = lax.Precision.HIGHEST
    pulled_disp = jnp.einsum("gpij,gpcj->gpci", weights, far_disp, precision=highest)
    pulled_vel = jnp.einsum("gpij,gpcj->gpci", weights, far_vel, precision=highest)
    pushed_disp = jnp.einsum("gpij,gci->gpcj", weights, own_disp, precision=highest)
    pushed_vel = jnp.einsum("gpij,gci->gpcj", weights, own_vel, precision=highest)
    stiff_coef = penalty / (8.0 * block_size)
    damp_coef = damping / (8.0 * block_size)
    row_wide = row_total[:, :, None, :]
    col_wide = col_total[:, :, None, :]
    action = jnp.sum(stiff_coef * (own_disp[:, None] * row_wide - pulled_disp)
                     + damp_coef * (pulled_vel - own_vel[:, None] * row_wide), axis=1)
    reaction = -(stiff_coef * (pushed_disp - far_disp * col_wide)
                 + damp_coef * (far_vel * col_wide - pushed_vel))
    return action, reaction


def internal_force(padded_disp, padded_stiff, displacement):
    size_x, size_z, size_y = displacement.shape[1:]
    corner_sum = jnp.zeros((3, size_x + 1, size_z + 1, size_y + 1), jnp.float32)
    for shift_x in (0, 1):
        for shift_z in (0, 1):
            for shift_y in (0, 1):
                corner_sum = corner_sum + padded_disp[:, shift_x:shift_x + size_x + 1, shift_z:shift_z + size_z + 1, shift_y:shift_y + size_y + 1]
    mean_disp = corner_sum / 8.0
    element_stiff = padded_stiff[:size_x + 1, :size_z + 1, :size_y + 1]
    weighted = element_stiff[None] * mean_disp
    node_stiff = jnp.zeros((size_x, size_z, size_y), jnp.float32)
    node_pull = jnp.zeros((3, size_x, size_z, size_y), jnp.float32)
    for shift_x in (0, 1):
        for shift_z in (0, 1):
            for shift_y in (0, 1):
                node_stiff = node_stiff + element_stiff[shift_x:shift_x + size_x, shift_z:shift_z + size_z, shift_y:shift_y + size_y]
                node_pull = node_pull + weighted[:, shift_x:shift_x + size_x, shift_z:shift_z + size_z, shift_y:shift_y + size_y]
    return node_pull - displacement * node_stiff


def contact_force(displacement, velocity, facing):
    count_x, count_z, count_y = displacement.shape[1:]
    groups = count_y // CY
    blocks = count_x * groups
    surface = jnp.concatenate([displacement[:, :, count_z - 1, :], velocity[:, :, count_z - 1, :]], axis=0)
    blocked = surface.reshape(6, count_x, groups, CY).transpose(1, 2, 0, 3).reshape(blocks, 6, CY)
    targets = facing.reshape(blocks, 8)
    batch_size = 32

    def visit_group(accumulated, group_index):
        first_row = group_index * batch_size
        own_block = lax.dynamic_slice_in_dim(blocked, first_row, batch_size, 0)
        chosen = lax.dynamic_slice_in_dim(targets, first_row, batch_size, 0)
        facing_blocks = blocked[chosen]
        action, reaction = pair_forces(own_block, facing_blocks)
        current = lax.dynamic_slice_in_dim(accumulated, first_row, batch_size, 0)
        accumulated = lax.dynamic_update_slice_in_dim(accumulated, current + action, first_row, 0)
        accumulated = accumulated.at[chosen.reshape(-1)].add(reaction.reshape(batch_size * 8, 3, CY))
        return accumulated, None

    start_total = jnp.zeros((blocks, 3, CY), jnp.float32)
    accumulated, _ = lax.scan(visit_group, start_total, jnp.arange(blocks // batch_size, dtype=jnp.int32))
    return accumulated.reshape(count_x, groups, 3, CY).transpose(2, 0, 1, 3).reshape(3, count_x, count_y)


def reference(displacement, velocity, stiffness, inverse_mass, facing):
    count_x, count_z, count_y = stiffness.shape
    inside = ((jnp.arange(count_x, dtype=jnp.int32) < count_x - 1)[:, None, None]
              & (jnp.arange(count_z, dtype=jnp.int32) < count_z - 1)[None, :, None]
              & (jnp.arange(count_y, dtype=jnp.int32) < count_y - 1)[None, None, :])
    masked_stiff = jnp.where(inside, stiffness, 0.0)
    padded_stiff = jnp.pad(masked_stiff, 1)
    for repeat in range(STEPS):
        padded_disp = jnp.pad(displacement, ((0, 0), (1, 1), (1, 1), (1, 1)))
        internal = internal_force(padded_disp, padded_stiff, displacement)
        contact = contact_force(displacement, velocity, facing)
        total_force = internal.at[:, :, count_z - 1, :].add(contact)
        velocity = velocity + time_step * inverse_mass[None] * total_force
        displacement = displacement + time_step * velocity
    return displacement, velocity
```

```python
import jax
import jax.numpy as jnp
import numpy as np
from jax import lax
from jax.experimental import pallas as pl
from jax.experimental.pallas import tpu as pltpu
from jax.sharding import PartitionSpec as P

STEPS = 2
AXES = ("gx", "gy")
NODES = 128
ROWS = 32
DEPTH = 5
FACES = 8
ENTRIES = ROWS * FACES
UNROLL = 4

time_step = 0.2
stiff_coef = 4.0 / (8.0 * NODES)
damp_coef = 1.0 / (8.0 * NODES)
exponent_scale = float(np.sqrt(np.log2(np.e) / 2.0))
frame_extent = 4.0

f32 = jnp.float32
bf16 = jnp.bfloat16
PARAMS = pltpu.CompilerParams(vmem_limit_bytes=48 * 1024 * 1024)


def sublanes(shape):
    return lax.broadcasted_iota(jnp.int32, shape, 0)


def lanes(shape):
    return lax.broadcasted_iota(jnp.int32, shape, 1)


def split3(value):
    high = value.astype(bf16).astype(f32)
    rest = value - high
    middle = rest.astype(bf16).astype(f32)
    return high, middle, rest - middle


def frame_tile():
    shape = (8, NODES)
    place = (lanes(shape).astype(f32) - (NODES - 1) / 2.0) * (frame_extent / NODES)
    return jnp.where(sublanes(shape) == 1, place, 0.0)


def tile_constants():
    row = sublanes((8, NODES))
    return frame_tile(), (row < 3).astype(f32), (row == 3).astype(f32), (row == 4).astype(f32)


def tile_parts(disp, vel, consts):
    frame, first3, row3, _ = consts
    place = disp + frame
    scaled = (place * exponent_scale) * first3
    half = 0.5 * jnp.sum(scaled * scaled, axis=0, keepdims=True)
    potential = (stiff_coef * place - damp_coef * vel) * first3 + row3
    return scaled, half, potential


def far_factor(scaled, half, consts):
    h, m, l = split3(scaled + half * consts[2] + consts[3])
    return jnp.concatenate([h, m, h, m, l, h], axis=0).astype(bf16)


def near_factor(scaled, half, consts):
    h, m, l = split3(scaled - consts[2] - half * consts[3])
    return jnp.concatenate([h, h, m, m, h, l], axis=0).astype(bf16)


def packed_potential(potential):
    h, m, l = split3(potential)
    return jnp.concatenate([h + pltpu.roll(m, 4, 0), l], axis=0).astype(bf16)


def fold(total):
    total = total[:8] + total[8:]
    return total + pltpu.roll(total, 4, 0)


def request_kernel(facing_ref, disp_ref, vel_ref, send_ref, slot_ref, surf_ref, count_ref):
    def clear(i, carry):
        count_ref[i] = 0
        return carry

    lax.fori_loop(0, NODES, clear, 0, unroll=16)
    zero = jnp.zeros((ROWS, NODES), f32)
    for c in range(3):
        surf_ref[:, c, :] = disp_ref[c]
        surf_ref[:, 3 + c, :] = vel_ref[c]
        if c < 2:
            surf_ref[:, 6 + c, :] = zero
    row6 = (sublanes((8, NODES)) == 6).astype(f32)

    def visit(b, carry):
        tile = surf_ref[b]
        for k in range(FACES):
            name = facing_ref[k, b]
            block = lax.shift_right_logical(name, 4)
            owner = lax.shift_left(lax.shift_right_logical(block, 5), 4) | (name & 15)
            used = count_ref[owner]
            count_ref[owner] = used + 1
            slot = 2 * owner + used
            slot_ref[b * FACES + k] = slot
            send_ref[slot] = tile + row6 * jnp.full((8, NODES), block & 31, jnp.int32).astype(f32)
        return carry

    lax.fori_loop(0, ROWS, visit, 0)


def edge_rows(value, x):
    return [value[c, z, x : x + 1, :] for c in range(value.shape[0]) for z in range(DEPTH)]


def edge_kernel(with_stiff, disp_ref, stiff_ref, last_ref, low_row, high_row, low_col, high_col, masked_ref):
    shape = (ROWS, NODES)
    lane = lanes(shape)
    if with_stiff:
        row = sublanes(shape)
        keep = ((row < ROWS - 1) | (last_ref[0] == 0)) & ((lane < NODES - 1) | (last_ref[1] == 0))
        for z in range(DEPTH):
            if z < DEPTH - 1:
                masked_ref[z] = jnp.where(keep, stiff_ref[z], 0.0)
            else:
                masked_ref[z] = jnp.zeros(shape, f32)
    low = jnp.zeros(shape, f32)
    high = jnp.zeros(shape, f32)
    low_row[...] = jnp.zeros((24, NODES), f32)
    high_row[...] = jnp.zeros((24, NODES), f32)
    for c in range(4 if with_stiff else 3):
        for z in range(DEPTH):
            at = c * DEPTH + z
            value = disp_ref[c, z] if c < 3 else masked_ref[z]
            low_row[at : at + 1, :] = value[0:1, :]
            high_row[at : at + 1, :] = value[ROWS - 1 :, :]
            low = jnp.where(lane == at, pltpu.roll(value, at, 1) if at else value, low)
            high = jnp.where(lane == at, pltpu.roll(value, at + 1, 1), high)
    low_col[...] = low
    high_col[...] = high


def extended(center, above, below):
    row = sublanes((8, NODES))
    tail = jnp.where(row == 0, below, jnp.where(row == 7, above, 0.0))
    return jnp.concatenate([center, tail], axis=0)


def force_kernel(with_stiff, disp_ref, stiff_ref, row_lo, row_hi, col_lo, col_hi, c_ll, c_hl, c_lh, c_hh, *rest):
    if with_stiff:
        surf_ref, force_ref, wide_ref, node_ref, near_ref, pot_ref, exact_ref = rest
    else:
        wide_in, node_in, surf_ref, force_ref, near_ref, pot_ref, exact_ref = rest
    wide = (ROWS + 8, NODES)
    lane = lanes(wide)
    last = lane == NODES - 1
    left = extended(col_lo[...], c_ll[7:8, :], c_hl[0:1, :])
    right = extended(col_hi[...], c_lh[7:8, :], c_hh[0:1, :])

    def own(c, z):
        value = disp_ref[c, z] if c < 3 else stiff_ref[z]
        at = c * DEPTH + z
        return extended(value, row_lo[at : at + 1, :], row_hi[at : at + 1, :])

    def at_last(cols, at):
        return pltpu.roll(cols, NODES - 1 - at, 1)

    def spread(main, side):
        main = main + pltpu.roll(main, 1, 0)
        side = side + pltpu.roll(side, 1, 0)
        return main + pltpu.roll(jnp.where(last, side, main), 1, 1)

    stiff = []
    if with_stiff:
        total = None
        for z in range(DEPTH - 1):
            main = own(3, z)
            side = at_last(left, 3 * DEPTH + z)
            wide_ref[z, 0] = main
            wide_ref[z, 1] = side
            stiff.append((main * 0.125, side * 0.125))
            out = spread(main, side)[:ROWS]
            node_ref[z] = out if total is None else total + out
            total = out
        node_ref[DEPTH - 1] = total
        node = node_ref
    else:
        for z in range(DEPTH - 1):
            stiff.append((wide_in[z, 0] * 0.125, wide_in[z, 1] * 0.125))
        node = node_in
    for c in range(3):
        boxes = []
        for z in range(DEPTH):
            value = own(c, z)
            turned = pltpu.roll(value, NODES - 1, 1)
            main = value + jnp.where(last, at_last(right, c * DEPTH + z), turned)
            side = at_last(left, c * DEPTH + z) + turned
            boxes.append((main, side))
        total = None
        for z in range(DEPTH):
            out = None
            if z < DEPTH - 1:
                main = boxes[z][0] + boxes[z + 1][0]
                side = boxes[z][1] + boxes[z + 1][1]
                main = main + pltpu.roll(main, ROWS + 7, 0)
                side = side + pltpu.roll(side, ROWS + 7, 0)
                out = spread(main * stiff[z][0], side * stiff[z][1])[:ROWS]
                pull = out if total is None else total + out
            else:
                pull = total
            total = out
            force_ref[c, z] = pull - disp_ref[c, z] * node[z]

    consts = tile_constants()
    unit = (lanes((NODES, NODES)) == sublanes((NODES, NODES))).astype(bf16)

    def table(b, carry):
        tile = surf_ref[b]
        scaled, half, potential = tile_parts(tile, pltpu.roll(tile, 5, 0), consts)
        near = near_factor(scaled, half, consts)
        turned = lax.dot_general(unit, near, (((1,), (1,)), ((), ())), preferred_element_type=f32)
        near_ref[b] = turned.astype(bf16)
        pot_ref[b] = packed_potential(potential)
        exact_ref[b] = potential
        return carry

    lax.fori_loop(0, ROWS, table, 0, unroll=4)


def contact_kernel(moved, row_ref, *rest):
    if moved:
        recv_ref, vel_ref, near_ref, pot_ref, out_ref, loc_ref = rest
    else:
        recv_ref, near_ref, pot_ref, out_ref, loc_ref = rest
    loc_ref[...] = jnp.zeros((ROWS, 8, NODES), f32)
    consts = tile_constants()

    def visit(step, carry):
        for j in range(UNROLL):
            e = step * UNROLL + j
            tile = recv_ref[e]
            if moved:
                vel = jnp.concatenate([vel_ref[e], jnp.zeros((4, NODES), f32)], axis=0)
                disp = tile + time_step * vel
            else:
                vel = pltpu.roll(tile, 5, 0)
                disp = tile
            scaled, half, potential = tile_parts(disp, vel, consts)
            far = far_factor(scaled, half, consts)
            far_pot = packed_potential(potential)
            r = row_ref[e]
            weight = jnp.exp2(jnp.dot(near_ref[r], far, preferred_element_type=f32))
            high = weight.astype(bf16)
            low = (weight - high.astype(f32)).astype(bf16)
            near_pot = pot_ref[r]
            pulled = fold(
                jnp.dot(
                    jnp.concatenate([near_pot, near_pot], axis=1),
                    jnp.concatenate([high, low], axis=0),
                    preferred_element_type=f32,
                )
            )
            out_ref[e] = (pulled[3:4] * potential - pulled)[:4]
            pushed = lax.dot_general(
                jnp.concatenate([far_pot, far_pot], axis=1),
                jnp.concatenate([high, low], axis=1),
                (((1,), (1,)), ((), ())),
                preferred_element_type=f32,
            )
            loc_ref[r] += pushed[:8] + pushed[8:]
        return carry

    lax.fori_loop(0, ENTRIES // UNROLL, visit, 0)


def update_kernel(
    final, slot_ref, ret_ref, loc_ref, exact_ref, force_ref, disp_ref, vel_ref, mass_ref, new_disp, new_vel, *rest
):
    if final:
        (sum_ref,) = rest
    else:
        send_ref, surf_ref, sum_ref = rest

    def gather(b, carry):
        total = loc_ref[b]
        total = total + pltpu.roll(total, 4, 0)
        acc = (total[3:4] * exact_ref[b] - total)[:4]
        for k in range(FACES):
            acc = acc + ret_ref[slot_ref[b * FACES + k]]
        sum_ref[b] = acc
        return carry

    lax.fori_loop(0, ROWS, gather, 0, unroll=4)
    if not final:
        for c in range(2):
            surf_ref[:, 6 + c, :] = jnp.zeros((ROWS, NODES), f32)
    for z in range(DEPTH):
        mass = time_step * mass_ref[z]
        for c in range(3):
            force = force_ref[c, z]
            if z == DEPTH - 1:
                force = force + sum_ref[:, c, :]
            vel = vel_ref[c, z] + mass * force
            disp = disp_ref[c, z] + time_step * vel
            new_vel[c, z] = vel
            new_disp[c, z] = disp
            if z == DEPTH - 1 and not final:
                surf_ref[:, c, :] = disp
                surf_ref[:, 3 + c, :] = vel
    if final:
        return

    def scatter(b, carry):
        tile = pltpu.roll(surf_ref[b], 5, 0)[:4]
        for k in range(FACES):
            send_ref[slot_ref[b * FACES + k]] = tile
        return carry

    lax.fori_loop(0, ROWS, scatter, 0, unroll=4)


VMEM = pl.BlockSpec(memory_space=pltpu.VMEM)
SMEM = pl.BlockSpec(memory_space=pltpu.SMEM)


def struct(*shape, dtype=f32):
    return jax.ShapeDtypeStruct(shape, dtype)


def shifted(value, count_gx, count_gy, dx, dy):
    pairs = []
    for x in range(count_gx):
        for y in range(count_gy):
            if 0 <= x + dx < count_gx and 0 <= y + dy < count_gy:
                pairs.append((x * count_gy + y, (x + dx) * count_gy + y + dy))
    return lax.ppermute(value, AXES, pairs)


def halo(edges, count_gx, count_gy):
    low_row, high_row, low_col, high_col = edges

    def go(value, dx, dy):
        return shifted(value, count_gx, count_gy, dx, dy)

    return (
        go(high_row, 1, 0),
        go(low_row, -1, 0),
        go(high_col, 0, 1),
        go(low_col, 0, -1),
        go(high_col[ROWS - 8 :], 1, 1),
        go(high_col[:8], -1, 1),
        go(low_col[ROWS - 8 :], 1, -1),
        go(low_col[:8], -1, -1),
    )


def local(displacement, velocity, stiffness, inverse_mass, facing):
    count_gx = lax.axis_size("gx")
    count_gy = lax.axis_size("gy")
    disp = displacement.transpose(0, 2, 1, 3)
    vel = velocity.transpose(0, 2, 1, 3)
    stiff = stiffness.transpose(1, 0, 2)
    mass = inverse_mass.transpose(1, 0, 2)
    faces = facing.transpose(1, 2, 0).reshape(FACES, ROWS)
    ends = jnp.stack(
        [
            (lax.axis_index("gx") == count_gx - 1).astype(jnp.int32),
            (lax.axis_index("gy") == count_gy - 1).astype(jnp.int32),
        ]
    )
    plane = (3, 1, ROWS, NODES)
    top = pl.BlockSpec((3, None, ROWS, NODES), lambda i: (0, DEPTH - 1, 0, 0))
    send, slots, surf = pl.pallas_call(
        request_kernel,
        grid=(1,),
        in_specs=[SMEM, top, top],
        out_specs=[VMEM, SMEM, VMEM],
        out_shape=[struct(ENTRIES, 8, NODES), struct(ENTRIES, dtype=jnp.int32), struct(ROWS, 8, NODES)],
        scratch_shapes=[pltpu.SMEM((NODES,), jnp.int32)],
        compiler_params=PARAMS,
        name="request",
    )(faces, disp, vel)
    first_recv = lax.all_to_all(send, AXES, 0, 0, tiled=True)
    wide = node = None
    edge_shapes = [struct(24, NODES), struct(24, NODES), struct(ROWS, NODES), struct(ROWS, NODES)]
    table_shapes = [
        struct(ROWS, NODES, 48, dtype=bf16),
        struct(ROWS, 16, NODES, dtype=bf16),
        struct(ROWS, 8, NODES),
    ]
    force_shape = [struct(3, DEPTH, ROWS, NODES)]
    for step in range(STEPS):
        if step == 0:
            *edges, masked = pl.pallas_call(
                lambda d, s, e, *outs: edge_kernel(True, d, s, e, *outs),
                in_specs=[VMEM, VMEM, SMEM],
                out_specs=[VMEM] * 5,
                out_shape=edge_shapes + [struct(DEPTH, ROWS, NODES)],
                compiler_params=PARAMS,
                name="edges_first",
            )(disp, stiff, ends)
            around = halo(edges, count_gx, count_gy)
            force, wide, node, near, pot, exact = pl.pallas_call(
                lambda *refs: force_kernel(True, *refs),
                in_specs=[VMEM] * 11,
                out_specs=[VMEM] * 6,
                out_shape=force_shape
                + [struct(DEPTH - 1, 2, ROWS + 8, NODES), struct(DEPTH, ROWS, NODES)]
                + table_shapes,
                compiler_params=PARAMS,
                name="force_first",
            )(disp, masked, *around, surf)
            rows = first_recv[:, 6, 0].astype(jnp.int32)
            extra = ()
        else:
            edges = pl.pallas_call(
                lambda d, *outs: edge_kernel(False, d, None, None, *outs, None),
                in_specs=[VMEM],
                out_specs=[VMEM] * 4,
                out_shape=edge_shapes,
                compiler_params=PARAMS,
                name="edges_next",
            )(disp)
            around = halo(edges, count_gx, count_gy)
            force, near, pot, exact = pl.pallas_call(
                lambda d, *refs: force_kernel(False, d, None, *refs),
                in_specs=[VMEM] * 12,
                out_specs=[VMEM] * 4,
                out_shape=force_shape + table_shapes,
                compiler_params=PARAMS,
                name="force_next",
            )(disp, *around, wide, node, surf)
            extra = (lax.all_to_all(send, AXES, 0, 0, tiled=True),)
        moved = step > 0
        action, reaction = pl.pallas_call(
            lambda *refs, moved=moved: contact_kernel(moved, *refs),
            in_specs=[SMEM] + [VMEM] * (3 + len(extra)),
            out_specs=[VMEM] * 2,
            out_shape=[struct(ENTRIES, 4, NODES), struct(ROWS, 8, NODES)],
            compiler_params=PARAMS,
            name="contact",
        )(rows, first_recv, *extra, near, pot)
        returned = lax.all_to_all(action, AXES, 0, 0, tiled=True)
        final = step == STEPS - 1
        outs = [struct(3, DEPTH, ROWS, NODES), struct(3, DEPTH, ROWS, NODES)]
        if not final:
            outs += [struct(ENTRIES, 4, NODES), struct(ROWS, 8, NODES)]
        disp, vel, *rest = pl.pallas_call(
            lambda *refs, final=final: update_kernel(final, *refs),
            in_specs=[SMEM] + [VMEM] * 7,
            out_specs=[VMEM] * len(outs),
            out_shape=outs,
            scratch_shapes=[pltpu.VMEM((ROWS, 4, NODES), f32)],
            compiler_params=PARAMS,
            name="update",
        )(slots, returned, reaction, exact, force, disp, vel, mass)
        if not final:
            send, surf = rest
    return disp.transpose(0, 2, 1, 3), vel.transpose(0, 2, 1, 3)


def solution(mesh):
    in_specs = (
        P(None, "gx", None, "gy"),
        P(None, "gx", None, "gy"),
        P("gx", None, "gy"),
        P("gx", None, "gy"),
        P("gx", "gy", None),
    )
    out_specs = (P(None, "gx", None, "gy"), P(None, "gx", None, "gy"))
    return jax.shard_map(local, mesh=mesh, in_specs=in_specs, out_specs=out_specs, check_vma=False)
```

```python
import jax
import jax.numpy as jnp
import numpy as np
from jax import lax
from jax.experimental import pallas as pl
from jax.experimental.pallas import tpu as pltpu
from jax.sharding import PartitionSpec as P

STEPS = 2
AXES = ("gx", "gy")
NODES = 128
ROWS = 32
DEPTH = 5
FACES = 8
ENTRIES = ROWS * FACES
UNROLL = 64
LAG = 7

time_step = 0.2
stiff_coef = 4.0 / (8.0 * NODES)
damp_coef = 1.0 / (8.0 * NODES)
exponent_scale = float(np.sqrt(np.log2(np.e) / 2.0))
frame_extent = 4.0

f32 = jnp.float32
bf16 = jnp.bfloat16
PARAMS = pltpu.CompilerParams(vmem_limit_bytes=48 * 1024 * 1024)


def sublanes(shape):
    return lax.broadcasted_iota(jnp.int32, shape, 0)


def lanes(shape):
    return lax.broadcasted_iota(jnp.int32, shape, 1)


def split3(value):
    high = value.astype(bf16).astype(f32)
    rest = value - high
    middle = rest.astype(bf16).astype(f32)
    return high, middle, rest - middle


def frame_tile():
    shape = (8, NODES)
    place = (lanes(shape).astype(f32) - (NODES - 1) / 2.0) * (frame_extent / NODES)
    return jnp.where(sublanes(shape) == 1, place, 0.0)


def tile_constants():
    row = sublanes((8, NODES))
    return frame_tile(), (row < 3).astype(f32), (row == 3).astype(f32), (row == 4).astype(f32)


def tile_parts(disp, vel, consts):
    frame, first3, row3, _ = consts
    place = disp + frame
    scaled = (place * exponent_scale) * first3
    half = 0.5 * jnp.sum(scaled * scaled, axis=0, keepdims=True)
    potential = (stiff_coef * place - damp_coef * vel) * first3 + row3
    return scaled, half, potential


def far_factor(scaled, half, consts):
    h, m, l = split3(scaled + half * consts[2] + consts[3])
    return jnp.concatenate([h, m, h, m, l, h], axis=0).astype(bf16)


def near_factor(scaled, half, consts):
    h, m, l = split3(scaled - consts[2] - half * consts[3])
    return jnp.concatenate([h, h, m, m, h, l], axis=0).astype(bf16)


def packed_potential(potential):
    h, m, l = split3(potential)
    return jnp.concatenate([h + pltpu.roll(m, 4, 0), l], axis=0).astype(bf16)


def fold(total):
    total = total[:8] + total[8:]
    return total + pltpu.roll(total, 4, 0)


def request_kernel(facing_hbm, disp_hbm, vel_hbm, send_ref, slot_ref, surf_ref, facing_ref, top_ref, count_ref, sems):
    copies = [
        pltpu.make_async_copy(disp_hbm.at[:, DEPTH - 1], top_ref.at[0], sems.at[0]),
        pltpu.make_async_copy(vel_hbm.at[:, DEPTH - 1], top_ref.at[1], sems.at[1]),
        pltpu.make_async_copy(facing_hbm, facing_ref, sems.at[2]),
    ]
    for copy in copies:
        copy.start()

    def clear(i, carry):
        count_ref[i] = 0
        return carry

    lax.fori_loop(0, NODES, clear, 0, unroll=16)
    for copy in copies:
        copy.wait()
    zero = jnp.zeros((ROWS, NODES), f32)
    for c in range(3):
        surf_ref[:, c, :] = top_ref[0, c]
        surf_ref[:, 3 + c, :] = top_ref[1, c]
        if c < 2:
            surf_ref[:, 6 + c, :] = zero
    row6 = (sublanes((8, NODES)) == 6).astype(f32)

    def visit(b, carry):
        tile = surf_ref[b]
        for k in range(FACES):
            name = facing_ref[k, b]
            block = lax.shift_right_logical(name, 4)
            owner = lax.shift_left(lax.shift_right_logical(block, 5), 4) | (name & 15)
            used = count_ref[owner]
            count_ref[owner] = used + 1
            slot = 2 * owner + used
            slot_ref[b * FACES + k] = slot
            send_ref[slot] = tile + row6 * jnp.full((8, NODES), block & 31, jnp.int32).astype(f32)
        return carry

    lax.fori_loop(0, ROWS, visit, 0)


def edge_rows(value, x):
    return [value[c, z, x : x + 1, :] for c in range(value.shape[0]) for z in range(DEPTH)]


def table_kernel(surf_ref, near_ref, pot_ref, exact_ref):
    consts = tile_constants()
    unit = (lanes((NODES, NODES)) == sublanes((NODES, NODES))).astype(bf16)

    def table(b, carry):
        tile = surf_ref[b]
        scaled, half, potential = tile_parts(tile, pltpu.roll(tile, 5, 0), consts)
        near = near_factor(scaled, half, consts)
        turned = lax.dot_general(unit, near, (((1,), (1,)), ((), ())), preferred_element_type=f32)
        near_ref[b] = turned.astype(bf16)
        pot_ref[b] = packed_potential(potential)
        exact_ref[b] = potential
        return carry

    lax.fori_loop(0, ROWS, table, 0, unroll=4)


def edge_kernel(with_stiff, *refs):
    if with_stiff:
        last_ref, disp_ref, surf_ref, stiff_ref, *refs = refs
        low_row, high_row, low_col, high_col, near_ref, pot_ref, exact_ref, masked_ref = refs
    else:
        disp_ref, surf_ref, low_row, high_row, low_col, high_col, near_ref, pot_ref, exact_ref = refs
    shape = (ROWS, NODES)
    lane = lanes(shape)
    if with_stiff:
        row = sublanes(shape)
        keep = ((row < ROWS - 1) | (last_ref[0] == 0)) & ((lane < NODES - 1) | (last_ref[1] == 0))
        for z in range(DEPTH):
            if z < DEPTH - 1:
                masked_ref[z] = jnp.where(keep, stiff_ref[z], 0.0)
            else:
                masked_ref[z] = jnp.zeros(shape, f32)
    low = jnp.zeros(shape, f32)
    high = jnp.zeros(shape, f32)
    low_row[...] = jnp.zeros((24, NODES), f32)
    high_row[...] = jnp.zeros((24, NODES), f32)
    for c in range(4 if with_stiff else 3):
        for z in range(DEPTH):
            at = c * DEPTH + z
            value = disp_ref[c, z] if c < 3 else masked_ref[z]
            low_row[at : at + 1, :] = value[0:1, :]
            high_row[at : at + 1, :] = value[ROWS - 1 :, :]
            low = jnp.where(lane == at, pltpu.roll(value, at, 1) if at else value, low)
            high = jnp.where(lane == at, pltpu.roll(value, at + 1, 1), high)
    low_col[...] = low
    high_col[...] = high
    table_kernel(surf_ref, near_ref, pot_ref, exact_ref)


def extended(center, above, below):
    row = sublanes((8, NODES))
    tail = jnp.where(row == 0, below, jnp.where(row == 7, above, 0.0))
    return jnp.concatenate([center, tail], axis=0)


def force_kernel(with_stiff, disp_ref, *refs):
    if with_stiff:
        stiff_ref, row_lo, row_hi, col_lo, col_hi, force_ref, wide_ref, node_ref = refs
    else:
        wide_in, node_in, row_lo, row_hi, col_lo, col_hi, force_ref = refs
    wide = (ROWS + 8, NODES)
    lane = lanes(wide)
    last = lane == NODES - 1
    left = extended(col_lo[...], row_lo[24:25, :], row_hi[24:25, :])
    right = extended(col_hi[...], row_lo[25:26, :], row_hi[25:26, :])

    def own(c, z):
        value = disp_ref[c, z] if c < 3 else stiff_ref[z]
        at = c * DEPTH + z
        return extended(value, row_lo[at : at + 1, :], row_hi[at : at + 1, :])

    def at_last(cols, at):
        return pltpu.roll(cols, NODES - 1 - at, 1)

    def spread(main, side):
        main = main + pltpu.roll(main, 1, 0)
        side = side + pltpu.roll(side, 1, 0)
        return main + pltpu.roll(jnp.where(last, side, main), 1, 1)

    stiff = []
    if with_stiff:
        total = None
        for z in range(DEPTH - 1):
            main = own(3, z)
            side = at_last(left, 3 * DEPTH + z)
            wide_ref[z, 0] = main
            wide_ref[z, 1] = side
            stiff.append((main * 0.125, side * 0.125))
            out = spread(main, side)[:ROWS]
            node_ref[z] = out if total is None else total + out
            total = out
        node_ref[DEPTH - 1] = total
        node = node_ref
    else:
        for z in range(DEPTH - 1):
            stiff.append((wide_in[z, 0] * 0.125, wide_in[z, 1] * 0.125))
        node = node_in
    for c in range(3):
        boxes = []
        for z in range(DEPTH):
            value = own(c, z)
            turned = pltpu.roll(value, NODES - 1, 1)
            main = value + jnp.where(last, at_last(right, c * DEPTH + z), turned)
            side = at_last(left, c * DEPTH + z) + turned
            boxes.append((main, side))
        total = None
        for z in range(DEPTH):
            out = None
            if z < DEPTH - 1:
                main = boxes[z][0] + boxes[z + 1][0]
                side = boxes[z][1] + boxes[z + 1][1]
                main = main + pltpu.roll(main, ROWS + 7, 0)
                side = side + pltpu.roll(side, ROWS + 7, 0)
                out = spread(main * stiff[z][0], side * stiff[z][1])[:ROWS]
                pull = out if total is None else total + out
            else:
                pull = total
            total = out
            force_ref[c, z] = pull - disp_ref[c, z] * node[z]


def entry_rows(recv_ref, turn_ref, row_ref, sem):
    shape = (NODES, NODES)
    diagonal = lanes(shape) == sublanes(shape)
    for half in range(ENTRIES // NODES):
        held = recv_ref[half * NODES : (half + 1) * NODES, 6, :]
        picked = jnp.sum(jnp.where(diagonal, held, 0.0), axis=0, keepdims=True)
        turn_ref[half : half + 1, :] = picked.astype(jnp.int32)
    copy = pltpu.make_async_copy(turn_ref, row_ref, sem)
    copy.start()
    copy.wait()


def contact_kernel(moved, *refs):
    if moved:
        row_in, recv_ref, vel_ref, near_ref, pot_ref, *refs = refs
    else:
        recv_ref, near_ref, pot_ref, *refs = refs
    low_row, high_row, col_lo, col_hi, *refs = refs
    if moved:
        out_ref, loc_ref, low_out, high_out = refs
        row_ref = row_in
    else:
        out_ref, loc_ref, low_out, high_out, row_ref, turn_ref, sem = refs
        entry_rows(recv_ref, turn_ref, row_ref, sem)
    for side, edge, at in ((low_out, low_row, 0), (high_out, high_row, ROWS - 1)):
        side[:24] = edge[...]
        side[24:25] = col_lo[at : at + 1, :]
        side[25:26] = col_hi[at : at + 1, :]
        side[26:] = jnp.zeros((ROWS - 26, NODES), f32)
    loc_ref[...] = jnp.zeros((ROWS, 8, NODES), f32)
    consts = tile_constants()

    def visit(step, carry):
        entries = [step * UNROLL + j for j in range(UNROLL)]
        first = step * UNROLL
        row = [row_ref[first // NODES, first % NODES + j] for j in range(UNROLL)]
        held = {}

        def weigh(j):
            tile = recv_ref[entries[j]]
            if moved:
                vel = jnp.concatenate([vel_ref[entries[j]], jnp.zeros((4, NODES), f32)], axis=0)
                disp = tile + time_step * vel
            else:
                vel = pltpu.roll(tile, 5, 0)
                disp = tile
            scaled, half, potential = tile_parts(disp, vel, consts)
            far = far_factor(scaled, half, consts)
            exponent = jnp.dot(near_ref[row[j]], far, preferred_element_type=f32)
            held[j] = exponent, packed_potential(potential), potential

        def reduce(j):
            exponent, far_pot, potential = held[j]
            weight = jnp.exp2(exponent)
            high = weight.astype(bf16)
            low = (weight - high.astype(f32)).astype(bf16)
            near_pot = pot_ref[row[j]]
            pulled = jnp.dot(
                jnp.concatenate([near_pot, near_pot], axis=1),
                jnp.concatenate([high, low], axis=0),
                preferred_element_type=f32,
            )
            pushed = lax.dot_general(
                jnp.concatenate([far_pot, far_pot], axis=1),
                jnp.concatenate([high, low], axis=1),
                (((1,), (1,)), ((), ())),
                preferred_element_type=f32,
            )
            held[j] = pulled, pushed, potential

        def store(j):
            pulled, pushed, potential = held.pop(j)
            pulled = fold(pulled)
            out_ref[entries[j]] = (pulled[3:4] * potential - pulled)[:4]
            loc_ref[row[j]] += pushed[:8] + pushed[8:]

        for t in range(UNROLL + LAG + 1):
            if t < UNROLL:
                weigh(t)
            if 0 <= t - LAG < UNROLL:
                reduce(t - LAG)
            if 0 <= t - LAG - 1 < UNROLL:
                store(t - LAG - 1)
        return carry

    lax.fori_loop(0, ENTRIES // UNROLL, visit, 0)


def update_kernel(
    final, slot_ref, ret_ref, loc_ref, exact_ref, force_ref, disp_ref, vel_ref, mass_ref, new_disp, new_vel, *rest
):
    if final:
        (sum_ref,) = rest
    else:
        send_ref, surf_ref, sum_ref = rest

    def gather(b, carry):
        total = loc_ref[b]
        total = total + pltpu.roll(total, 4, 0)
        acc = (total[3:4] * exact_ref[b] - total)[:4]
        for k in range(FACES):
            acc = acc + ret_ref[slot_ref[b * FACES + k]]
        sum_ref[b] = acc
        return carry

    lax.fori_loop(0, ROWS, gather, 0, unroll=4)
    if not final:
        for c in range(2):
            surf_ref[:, 6 + c, :] = jnp.zeros((ROWS, NODES), f32)
    for z in range(DEPTH):
        mass = time_step * mass_ref[z]
        for c in range(3):
            force = force_ref[c, z]
            if z == DEPTH - 1:
                force = force + sum_ref[:, c, :]
            vel = vel_ref[c, z] + mass * force
            disp = disp_ref[c, z] + time_step * vel
            new_vel[c, z] = vel
            new_disp[c, z] = disp
            if z == DEPTH - 1 and not final:
                surf_ref[:, c, :] = disp
                surf_ref[:, 3 + c, :] = vel
    if final:
        return

    def scatter(b, carry):
        tile = pltpu.roll(surf_ref[b], 5, 0)[:4]
        for k in range(FACES):
            send_ref[slot_ref[b * FACES + k]] = tile
        return carry

    lax.fori_loop(0, ROWS, scatter, 0, unroll=4)


VMEM = pl.BlockSpec(memory_space=pltpu.VMEM)
SMEM = pl.BlockSpec(memory_space=pltpu.SMEM)
ANY = pl.BlockSpec(memory_space=pl.ANY)


def struct(*shape, dtype=f32):
    return jax.ShapeDtypeStruct(shape, dtype)


def shifted(value, count_gx, count_gy, dx, dy):
    pairs = []
    for x in range(count_gx):
        for y in range(count_gy):
            if 0 <= x + dx < count_gx and 0 <= y + dy < count_gy:
                pairs.append((x * count_gy + y, (x + dx) * count_gy + y + dy))
    return lax.ppermute(value, AXES, pairs)


def local(displacement, velocity, stiffness, inverse_mass, facing):
    count_gx = lax.axis_size("gx")
    count_gy = lax.axis_size("gy")
    disp = displacement.transpose(0, 2, 1, 3)
    vel = velocity.transpose(0, 2, 1, 3)
    stiff = stiffness.transpose(1, 0, 2)
    mass = inverse_mass.transpose(1, 0, 2)
    faces = facing.transpose(1, 2, 0).reshape(FACES, ROWS)
    ends = jnp.stack(
        [
            (lax.axis_index("gx") == count_gx - 1).astype(jnp.int32),
            (lax.axis_index("gy") == count_gy - 1).astype(jnp.int32),
        ]
    )
    send, slots, surf = pl.pallas_call(
        request_kernel,
        in_specs=[ANY] * 3,
        out_specs=[VMEM, SMEM, VMEM],
        out_shape=[struct(ENTRIES, 8, NODES), struct(ENTRIES, dtype=jnp.int32), struct(ROWS, 8, NODES)],
        scratch_shapes=[
            pltpu.SMEM((FACES, ROWS), jnp.int32),
            pltpu.VMEM((2, 3, ROWS, NODES), f32),
            pltpu.SMEM((NODES,), jnp.int32),
            pltpu.SemaphoreType.DMA((3,)),
        ],
        compiler_params=PARAMS,
        name="request",
    )(faces, disp, vel)
    wide = node = rows = first_recv = masked = None
    edge_shapes = [
        struct(24, NODES),
        struct(24, NODES),
        struct(ROWS, NODES),
        struct(ROWS, NODES),
        struct(ROWS, NODES, 48, dtype=bf16),
        struct(ROWS, 16, NODES, dtype=bf16),
        struct(ROWS, 8, NODES),
    ]
    force_shape = [struct(3, DEPTH, ROWS, NODES)]

    def go(value, dx, dy):
        return shifted(value, count_gx, count_gy, dx, dy)

    for step in range(STEPS):
        moved = step > 0
        recv = lax.all_to_all(send, AXES, 0, 0, tiled=True)
        if moved:
            outs = pl.pallas_call(
                lambda *refs: edge_kernel(False, *refs),
                in_specs=[VMEM] * 2,
                out_specs=[VMEM] * 7,
                out_shape=edge_shapes,
                compiler_params=PARAMS,
                name="edges_next",
            )(disp, surf)
        else:
            *outs, masked = pl.pallas_call(
                lambda *refs: edge_kernel(True, *refs),
                in_specs=[SMEM] + [VMEM] * 3,
                out_specs=[VMEM] * 8,
                out_shape=edge_shapes + [struct(DEPTH, ROWS, NODES)],
                compiler_params=PARAMS,
                name="edges_first",
            )(ends, disp, surf, stiff)
        low_row, high_row, low_col, high_col, near, pot, exact = outs
        col_lo = go(high_col, 0, 1)
        col_hi = go(low_col, 0, -1)
        shapes = [struct(ENTRIES, 4, NODES), struct(ROWS, 8, NODES), struct(ROWS, NODES), struct(ROWS, NODES)]
        edges = (low_row, high_row, col_lo, col_hi)
        if moved:
            action, reaction, low_out, high_out = pl.pallas_call(
                lambda *refs: contact_kernel(True, *refs),
                in_specs=[SMEM] + [VMEM] * 8,
                out_specs=[VMEM] * 4,
                out_shape=shapes,
                compiler_params=PARAMS,
                name="contact_next",
            )(rows, first_recv, recv, near, pot, *edges)
        else:
            first_recv = recv
            action, reaction, low_out, high_out, rows = pl.pallas_call(
                lambda *refs: contact_kernel(False, *refs),
                in_specs=[VMEM] * 7,
                out_specs=[VMEM] * 4 + [SMEM],
                out_shape=shapes + [struct(ENTRIES // NODES, NODES, dtype=jnp.int32)],
                scratch_shapes=[pltpu.VMEM((ENTRIES // NODES, NODES), jnp.int32), pltpu.SemaphoreType.DMA(())],
                compiler_params=PARAMS,
                name="contact_first",
            )(recv, near, pot, *edges)
        returned = lax.all_to_all(action, AXES, 0, 0, tiled=True)
        row_lo = go(high_out, 1, 0)
        row_hi = go(low_out, -1, 0)
        if moved:
            (force,) = pl.pallas_call(
                lambda *refs: force_kernel(False, *refs),
                in_specs=[VMEM] * 7,
                out_specs=[VMEM],
                out_shape=force_shape,
                compiler_params=PARAMS,
                name="force_next",
            )(disp, wide, node, row_lo, row_hi, col_lo, col_hi)
        else:
            force, wide, node = pl.pallas_call(
                lambda *refs: force_kernel(True, *refs),
                in_specs=[VMEM] * 6,
                out_specs=[VMEM] * 3,
                out_shape=force_shape + [struct(DEPTH - 1, 2, ROWS + 8, NODES), struct(DEPTH, ROWS, NODES)],
                compiler_params=PARAMS,
                name="force_first",
            )(disp, masked, row_lo, row_hi, col_lo, col_hi)
        final = step == STEPS - 1
        outs = [struct(3, DEPTH, ROWS, NODES), struct(3, DEPTH, ROWS, NODES)]
        if not final:
            outs += [struct(ENTRIES, 4, NODES), struct(ROWS, 8, NODES)]
        disp, vel, *rest = pl.pallas_call(
            lambda *refs, final=final: update_kernel(final, *refs),
            in_specs=[SMEM] + [VMEM] * 7,
            out_specs=[VMEM] * len(outs),
            out_shape=outs,
            scratch_shapes=[pltpu.VMEM((ROWS, 4, NODES), f32)],
            compiler_params=PARAMS,
            name="update",
        )(slots, returned, reaction, exact, force, disp, vel, mass)
        if not final:
            send, surf = rest
    return disp.transpose(0, 2, 1, 3), vel.transpose(0, 2, 1, 3)


def solution(mesh):
    in_specs = (
        P(None, "gx", None, "gy"),
        P(None, "gx", None, "gy"),
        P("gx", None, "gy"),
        P("gx", None, "gy"),
        P("gx", "gy", None),
    )
    out_specs = (P(None, "gx", None, "gy"), P(None, "gx", None, "gy"))
    return jax.shard_map(local, mesh=mesh, in_specs=in_specs, out_specs=out_specs, check_vma=False)
```

```python
import jax
import jax.numpy as jnp
import numpy as np
from jax import lax
from jax.experimental import pallas as pl
from jax.experimental.pallas import tpu as pltpu
from jax.sharding import PartitionSpec as P

AXES = ("gx", "gy")
NODES = 128
ROWS = 32
DEPTH = 5
FACES = 8
ENTRIES = ROWS * FACES
UNROLL = 64
LAG = 7

time_step = 0.2
stiff_coef = 4.0 / (8.0 * NODES)
damp_coef = 1.0 / (8.0 * NODES)
exponent_scale = float(np.sqrt(np.log2(np.e) / 2.0))
frame_extent = 4.0

f32 = jnp.float32
bf16 = jnp.bfloat16
PARAMS = pltpu.CompilerParams(vmem_limit_bytes=16 * 1024 * 1024)


def sublanes(shape):
    return lax.broadcasted_iota(jnp.int32, shape, 0)


def lanes(shape):
    return lax.broadcasted_iota(jnp.int32, shape, 1)


def split3(value):
    high = value.astype(bf16).astype(f32)
    rest = value - high
    middle = rest.astype(bf16).astype(f32)
    return high, middle, rest - middle


def frame_tile():
    shape = (8, NODES)
    place = (lanes(shape).astype(f32) - (NODES - 1) / 2.0) * (frame_extent / NODES)
    return jnp.where(sublanes(shape) == 1, place, 0.0)


def tile_constants():
    row = sublanes((8, NODES))
    return frame_tile(), (row < 3).astype(f32), (row == 3).astype(f32), (row == 4).astype(f32)


def tile_parts(disp, vel, consts):
    frame, first3, row3, _ = consts
    place = disp + frame
    scaled = (place * exponent_scale) * first3
    half = 0.5 * jnp.sum(scaled * scaled, axis=0, keepdims=True)
    potential = (stiff_coef * place - damp_coef * vel) * first3 + row3
    return scaled, half, potential


def far_factor(scaled, half, consts):
    h, m, l = split3(scaled + half * consts[2] + consts[3])
    return jnp.concatenate([h, m, h, m, l, h], axis=0).astype(bf16)


def near_factor(scaled, half, consts):
    h, m, l = split3(scaled - consts[2] - half * consts[3])
    return jnp.concatenate([h, h, m, m, h, l], axis=0).astype(bf16)


def packed_potential(potential):
    h, m, l = split3(potential)
    return jnp.concatenate([h + pltpu.roll(m, 4, 0), l], axis=0).astype(bf16)


def fold(total):
    total = total[:8] + total[8:]
    return total + pltpu.roll(total, 4, 0)


def request_kernel(facing_hbm, disp_hbm, vel_hbm, send_ref, slot_ref, home_ref, surf_ref, facing_ref, top_ref, count_ref, sems):
    copies = [
        pltpu.make_async_copy(disp_hbm.at[:, DEPTH - 1], top_ref.at[0], sems.at[0]),
        pltpu.make_async_copy(vel_hbm.at[:, DEPTH - 1], top_ref.at[1], sems.at[1]),
        pltpu.make_async_copy(facing_hbm, facing_ref, sems.at[2]),
    ]
    for copy in copies:
        copy.start()

    def clear(i, carry):
        count_ref[i] = 0
        return carry

    lax.fori_loop(0, NODES, clear, 0, unroll=16)
    for copy in copies:
        copy.wait()
    zero = jnp.zeros((ROWS, NODES), f32)
    for c in range(3):
        surf_ref[:, c, :] = top_ref[0, c]
        surf_ref[:, 3 + c, :] = top_ref[1, c]
        if c < 2:
            surf_ref[:, 6 + c, :] = zero
    row6 = (sublanes((8, NODES)) == 6).astype(f32)

    def visit(b, carry):
        tile = surf_ref[b]
        for k in range(FACES):
            name = facing_ref[k, b]
            block = lax.shift_right_logical(name, 4)
            owner = lax.shift_left(lax.shift_right_logical(block, 5), 4) | (name & 15)
            used = count_ref[owner]
            count_ref[owner] = used + 1
            slot = 2 * owner + used
            slot_ref[b * FACES + k] = slot
            home_ref[slot] = b
            send_ref[slot] = tile + row6 * jnp.full((8, NODES), block & 31, jnp.int32).astype(f32)
        return carry

    lax.fori_loop(0, ROWS, visit, 0)


def edge_rows(value, x):
    return [value[c, z, x : x + 1, :] for c in range(value.shape[0]) for z in range(DEPTH)]


def table_kernel(surf_ref, near_ref, exact_ref, pot_ref=None, tail_ref=None):
    consts = tile_constants()
    unit = (lanes((NODES, NODES)) == sublanes((NODES, NODES))).astype(bf16)

    def table(b, carry):
        tile = surf_ref[b]
        scaled, half, potential = tile_parts(tile, pltpu.roll(tile, 5, 0), consts)
        near = near_factor(scaled, half, consts)
        turned = lax.dot_general(unit, near, (((1,), (1,)), ((), ())), preferred_element_type=f32)
        near_ref[b] = turned.astype(bf16)
        exact_ref[b] = potential
        if pot_ref is not None:
            pot_ref[b] = packed_potential(potential)
            tail_ref[b] = (pltpu.roll(tile, 3, 0) * consts[2])[:4]
        return carry

    lax.fori_loop(0, ROWS, table, 0, unroll=4)


def edge_kernel(with_stiff, *refs):
    if with_stiff:
        last_ref, disp_ref, surf_ref, stiff_ref, *refs = refs
        low_row, high_row, low_col, high_col, near_ref, exact_ref, pot_ref, tail_ref, masked_ref = refs
    else:
        disp_ref, surf_ref, low_row, high_row, low_col, high_col, near_ref, exact_ref = refs
    shape = (ROWS, NODES)
    lane = lanes(shape)
    if with_stiff:
        row = sublanes(shape)
        keep = ((row < ROWS - 1) | (last_ref[0] == 0)) & ((lane < NODES - 1) | (last_ref[1] == 0))
        for z in range(DEPTH):
            if z < DEPTH - 1:
                masked_ref[z] = jnp.where(keep, stiff_ref[z], 0.0)
            else:
                masked_ref[z] = jnp.zeros(shape, f32)
    low = jnp.zeros(shape, f32)
    high = jnp.zeros(shape, f32)
    low_row[...] = jnp.zeros((24, NODES), f32)
    high_row[...] = jnp.zeros((24, NODES), f32)
    for c in range(4 if with_stiff else 3):
        for z in range(DEPTH):
            at = c * DEPTH + z
            value = disp_ref[c, z] if c < 3 else masked_ref[z]
            low_row[at : at + 1, :] = value[0:1, :]
            high_row[at : at + 1, :] = value[ROWS - 1 :, :]
            low = jnp.where(lane == at, pltpu.roll(value, at, 1) if at else value, low)
            high = jnp.where(lane == at, pltpu.roll(value, at + 1, 1), high)
    low_col[...] = low
    high_col[...] = high
    if with_stiff:
        table_kernel(surf_ref, near_ref, exact_ref, pot_ref, tail_ref)
    else:
        table_kernel(surf_ref, near_ref, exact_ref)


def extended(center, above, below):
    row = sublanes((8, NODES))
    tail = jnp.where(row == 0, below, jnp.where(row == 7, above, 0.0))
    return jnp.concatenate([center, tail], axis=0)


def force_kernel(with_stiff, disp_ref, *refs):
    if with_stiff:
        stiff_ref, row_lo, row_hi, col_lo, col_hi, force_ref, wide_ref, node_ref = refs
    else:
        wide_in, node_in, row_lo, row_hi, col_lo, col_hi, put = refs
    wide = (ROWS + 8, NODES)
    lane = lanes(wide)
    last = lane == NODES - 1
    left = extended(col_lo[...], row_lo[24:25, :], row_hi[24:25, :])
    right = extended(col_hi[...], row_lo[25:26, :], row_hi[25:26, :])

    def own(c, z):
        value = disp_ref[c, z] if c < 3 else stiff_ref[z]
        at = c * DEPTH + z
        return extended(value, row_lo[at : at + 1, :], row_hi[at : at + 1, :])

    def at_last(cols, at):
        return pltpu.roll(cols, NODES - 1 - at, 1)

    def spread(main, side):
        main = main + pltpu.roll(main, 1, 0)
        side = side + pltpu.roll(side, 1, 0)
        return main + pltpu.roll(jnp.where(last, side, main), 1, 1)

    stiff = []
    if with_stiff:
        total = None
        for z in range(DEPTH - 1):
            main = own(3, z)
            side = at_last(left, 3 * DEPTH + z)
            wide_ref[z, 0] = main
            wide_ref[z, 1] = side
            stiff.append((main * 0.125, side * 0.125))
            out = spread(main, side)[:ROWS]
            node_ref[z] = out if total is None else total + out
            total = out
        node_ref[DEPTH - 1] = total
        node = node_ref
    else:
        for z in range(DEPTH - 1):
            stiff.append((wide_in[z, 0] * 0.125, wide_in[z, 1] * 0.125))
        node = node_in
    for c in range(3):
        boxes = []
        for z in range(DEPTH):
            value = own(c, z)
            turned = pltpu.roll(value, NODES - 1, 1)
            main = value + jnp.where(last, at_last(right, c * DEPTH + z), turned)
            side = at_last(left, c * DEPTH + z) + turned
            boxes.append((main, side))
        total = None
        for z in range(DEPTH):
            out = None
            if z < DEPTH - 1:
                main = boxes[z][0] + boxes[z + 1][0]
                side = boxes[z][1] + boxes[z + 1][1]
                main = main + pltpu.roll(main, ROWS + 7, 0)
                side = side + pltpu.roll(side, ROWS + 7, 0)
                out = spread(main * stiff[z][0], side * stiff[z][1])[:ROWS]
                pull = out if total is None else total + out
            else:
                pull = total
            total = out
            force = pull - disp_ref[c, z] * node[z]
            if with_stiff:
                force_ref[c, z] = force
            else:
                put(c, z, force)


def entry_rows(recv_ref, turn_ref, row_ref, sem):
    shape = (NODES, NODES)
    diagonal = lanes(shape) == sublanes(shape)
    for half in range(ENTRIES // NODES):
        held = recv_ref[half * NODES : (half + 1) * NODES, 6, :]
        picked = jnp.sum(jnp.where(diagonal, held, 0.0), axis=0, keepdims=True)
        turn_ref[half : half + 1, :] = picked.astype(jnp.int32)
    copy = pltpu.make_async_copy(turn_ref, row_ref, sem)
    copy.start()
    copy.wait()


def row_messages(low_row, high_row, col_lo, col_hi, low_out, high_out):
    for side, edge, at in ((low_out, low_row, 0), (high_out, high_row, ROWS - 1)):
        side[:24] = edge[...]
        side[24:25] = col_lo[at : at + 1, :]
        side[25:26] = col_hi[at : at + 1, :]
        side[26:] = jnp.zeros((ROWS - 26, NODES), f32)


def pair_loop(row_of, tile_of, near_ref, loc_ref, pot_ref=None, tail_ref=None, out_ref=None):
    consts = tile_constants()

    def visit(step, carry):
        entries = [step * UNROLL + j for j in range(UNROLL)]
        row = [row_of(step, j) for j in range(UNROLL)]
        held = {}

        def weigh(j):
            scaled, half, potential = tile_parts(*tile_of(entries[j]), consts)
            far = far_factor(scaled, half, consts)
            exponent = jnp.dot(near_ref[row[j]], far, preferred_element_type=f32)
            held[j] = exponent, packed_potential(potential), potential

        def reduce(j):
            exponent, far_pot, potential = held[j]
            weight = jnp.exp2(exponent)
            high = weight.astype(bf16)
            low = (weight - high.astype(f32)).astype(bf16)
            pulled = None
            if out_ref is not None:
                near_pot = pot_ref[row[j]]
                pulled = jnp.dot(
                    jnp.concatenate([near_pot, near_pot], axis=1),
                    jnp.concatenate([high, low], axis=0),
                    preferred_element_type=f32,
                )
            pushed = lax.dot_general(
                jnp.concatenate([far_pot, far_pot], axis=1),
                jnp.concatenate([high, low], axis=1),
                (((1,), (1,)), ((), ())),
                preferred_element_type=f32,
            )
            held[j] = pulled, pushed, potential

        def store(j):
            pulled, pushed, potential = held.pop(j)
            if out_ref is not None:
                pulled = fold(pulled)
                out_ref[entries[j]] = (pulled[3:4] * potential - pulled)[:4] + tail_ref[row[j]]
            loc_ref[row[j]] += pushed[:8] + pushed[8:]

        for t in range(UNROLL + LAG + 1):
            if t < UNROLL:
                weigh(t)
            if 0 <= t - LAG < UNROLL:
                reduce(t - LAG)
            if 0 <= t - LAG - 1 < UNROLL:
                store(t - LAG - 1)
        return carry

    lax.fori_loop(0, ENTRIES // UNROLL, visit, 0)


def split_row(row_ref):
    def row_of(step, j):
        first = step * UNROLL
        return row_ref[first // NODES, first % NODES + j]

    return row_of


def wide_tile(value):
    return jnp.concatenate([value, jnp.zeros((4, NODES), f32)], axis=0)


def contact_first(recv_ref, near_ref, pot_ref, tail_ref, low_row, high_row, col_lo, col_hi, *refs):
    out_ref, loc_ref, low_out, high_out, row_ref, turn_ref, sem = refs
    entry_rows(recv_ref, turn_ref, row_ref, sem)
    row_messages(low_row, high_row, col_lo, col_hi, low_out, high_out)
    loc_ref[...] = jnp.zeros((ROWS, 8, NODES), f32)

    def tile_of(e):
        tile = recv_ref[e]
        return tile, pltpu.roll(tile, 5, 0)

    pair_loop(split_row(row_ref), tile_of, near_ref, loc_ref, pot_ref, tail_ref, out_ref)


def contact_last(row_ref, home_ref, first_ref, x_ref, new_ref, near_ref, loc_ref):
    loc_ref[...] = jnp.zeros((ROWS, 8, NODES), f32)
    row = sublanes((8, NODES))

    def faced(e):
        vel = new_ref[e]
        return first_ref[e] + time_step * vel, vel

    def facing(e):
        tile = new_ref[e]
        vel = pltpu.roll(tile, 4, 0)
        x = pltpu.roll(wide_tile(x_ref[e]), 5, 0)
        y = pltpu.roll(tile, 6, 0)
        z = pltpu.roll(tile, 3, 0)
        disp = jnp.where(row == 0, x, jnp.where(row == 1, y, z))
        return disp + time_step * vel, vel

    pair_loop(split_row(row_ref), faced, near_ref, loc_ref)
    pair_loop(lambda step, j: home_ref[step * UNROLL + j], facing, near_ref, loc_ref)


def local_sum(loc_ref, exact_ref, b):
    total = loc_ref[b]
    total = total + pltpu.roll(total, 4, 0)
    return (total[3:4] * exact_ref[b] - total)[:4]


def update_kernel(
    slot_ref, home_ref, row_ref, ret_ref, loc_ref, exact_ref, force_ref, disp_ref, vel_ref, mass_ref, old_ref, *refs
):
    new_disp, new_vel, send_ref, surf_ref, sum_ref, facing_tile, faced_tile = refs

    def gather(b, carry):
        acc = local_sum(loc_ref, exact_ref, b)
        for k in range(FACES):
            acc = acc + ret_ref[slot_ref[b * FACES + k]]
        sum_ref[b] = acc
        return carry

    lax.fori_loop(0, ROWS, gather, 0, unroll=4)
    for c in range(2):
        surf_ref[:, 6 + c, :] = jnp.zeros((ROWS, NODES), f32)
    for z in reversed(range(DEPTH)):
        mass = time_step * mass_ref[z]
        for c in range(3):
            force = force_ref[c, z]
            if z == DEPTH - 1:
                force = force + sum_ref[:, c, :]
            vel = vel_ref[c, z] + mass * force
            disp = disp_ref[c, z] + time_step * vel
            new_vel[c, z] = vel
            new_disp[c, z] = disp
            if z == DEPTH - 1:
                surf_ref[:, c, :] = disp
                surf_ref[:, 3 + c, :] = vel
    row = sublanes((8, NODES))

    def tiles(b, carry):
        tile = surf_ref[b]
        vel = pltpu.roll(tile, 5, 0)
        old = old_ref[b]
        facing_tile[b] = jnp.where(row < 3, vel, 0.0)
        late = jnp.where(row < 7, pltpu.roll(tile, 1, 0), pltpu.roll(old, 5, 0))
        faced_tile[b] = jnp.where(row < 3, 0.0, jnp.where(row == 3, pltpu.roll(old, 2, 0), late))
        return carry

    lax.fori_loop(0, ROWS, tiles, 0, unroll=8)

    def scatter(i, carry):
        for j in range(16):
            e = i * 16 + j
            r = row_ref[i * 16 // NODES, i * 16 % NODES + j]
            send_ref[e] = facing_tile[home_ref[e]] + faced_tile[r]
        return carry

    lax.fori_loop(0, ENTRIES // 16, scatter, 0)


def final_kernel(
    disp_ref, vel_ref, mass_ref, loc_ref, exact_ref, wide_in, node_in, row_lo, row_hi, col_lo, col_hi, *refs
):
    new_disp, new_vel, sum_ref = refs

    def gather(b, carry):
        sum_ref[b] = local_sum(loc_ref, exact_ref, b)
        return carry

    lax.fori_loop(0, ROWS, gather, 0, unroll=8)

    def put(c, z, force):
        if z == DEPTH - 1:
            force = force + sum_ref[:, c, :]
        vel = vel_ref[c, z] + time_step * mass_ref[z] * force
        new_vel[c, z] = vel
        new_disp[c, z] = disp_ref[c, z] + time_step * vel

    force_kernel(False, disp_ref, wide_in, node_in, row_lo, row_hi, col_lo, col_hi, put)


VMEM = pl.BlockSpec(memory_space=pltpu.VMEM)
SMEM = pl.BlockSpec(memory_space=pltpu.SMEM)
HBM = pl.BlockSpec(memory_space=pltpu.HBM)


def struct(*shape, dtype=f32):
    return jax.ShapeDtypeStruct(shape, dtype)


def shifted(value, count_gx, count_gy, dx, dy):
    pairs = []
    for x in range(count_gx):
        for y in range(count_gy):
            if 0 <= x + dx < count_gx and 0 <= y + dy < count_gy:
                pairs.append((x * count_gy + y, (x + dx) * count_gy + y + dy))
    return lax.ppermute(value, AXES, pairs)


def scalars(value):
    return pltpu.with_memory_space_constraint(value, pltpu.SMEM)


def local(displacement, velocity, stiffness, inverse_mass, facing):
    count_gx = lax.axis_size("gx")
    count_gy = lax.axis_size("gy")
    disp = displacement.transpose(0, 2, 1, 3)
    vel = velocity.transpose(0, 2, 1, 3)
    stiff = stiffness.transpose(1, 0, 2)
    mass = inverse_mass.transpose(1, 0, 2)
    faces = facing.transpose(1, 2, 0).reshape(FACES, ROWS)
    ends = jnp.stack(
        [
            (lax.axis_index("gx") == count_gx - 1).astype(jnp.int32),
            (lax.axis_index("gy") == count_gy - 1).astype(jnp.int32),
        ]
    )
    send, slots, homes, surf = pl.pallas_call(
        request_kernel,
        in_specs=[HBM] * 3,
        out_specs=[VMEM, SMEM, SMEM, VMEM],
        out_shape=[
            struct(ENTRIES, 8, NODES),
            pltpu.SMEM((ENTRIES,), jnp.int32),
            pltpu.SMEM((ENTRIES,), jnp.int32),
            struct(ROWS, 8, NODES),
        ],
        scratch_shapes=[
            pltpu.SMEM((FACES, ROWS), jnp.int32),
            pltpu.VMEM((2, 3, ROWS, NODES), f32),
            pltpu.SMEM((NODES,), jnp.int32),
            pltpu.SemaphoreType.DMA((3,)),
        ],
        compiler_params=PARAMS,
        name="request",
    )(*(pltpu.with_memory_space_constraint(value, pltpu.HBM) for value in (faces, disp, vel)))
    near_shape = struct(ROWS, NODES, 48, dtype=bf16)
    tile_shape = struct(ROWS, 8, NODES)
    small_shape = struct(ROWS, 4, NODES)
    edge_shape = struct(ROWS, NODES)
    edge_shapes = [struct(24, NODES), struct(24, NODES), edge_shape, edge_shape, near_shape, tile_shape]
    field_shape = struct(3, DEPTH, ROWS, NODES)
    entry_shape = struct(ENTRIES, 4, NODES)

    def go(value, dx, dy):
        return shifted(value, count_gx, count_gy, dx, dy)

    def exchange(value):
        return lax.all_to_all(value, AXES, 0, 0, tiled=True)

    def call(kernel, name, in_specs, out_specs, out_shape, scratch=()):
        return pl.pallas_call(
            kernel,
            in_specs=in_specs,
            out_specs=out_specs,
            out_shape=out_shape,
            scratch_shapes=scratch,
            compiler_params=PARAMS,
            name=name,
        )

    first = exchange(send)
    low_row, high_row, low_col, high_col, near, exact, pot, tail, masked = call(
        lambda *refs: edge_kernel(True, *refs),
        "edges_first",
        [SMEM] + [VMEM] * 3,
        [VMEM] * 9,
        edge_shapes + [struct(ROWS, 16, NODES, dtype=bf16), small_shape, struct(DEPTH, ROWS, NODES)],
    )(ends, disp, surf, stiff)
    col_lo = go(high_col, 0, 1)
    col_hi = go(low_col, 0, -1)
    action, reaction, low_out, high_out, rows = call(
        contact_first,
        "contact_first",
        [VMEM] * 8,
        [VMEM] * 4 + [SMEM],
        [entry_shape, tile_shape, edge_shape, edge_shape, pltpu.SMEM((ENTRIES // NODES, NODES), jnp.int32)],
        [pltpu.VMEM((ENTRIES // NODES, NODES), jnp.int32), pltpu.SemaphoreType.DMA(())],
    )(first, near, pot, tail, low_row, high_row, col_lo, col_hi)
    returned = exchange(action)
    row_lo = go(high_out, 1, 0)
    row_hi = go(low_out, -1, 0)
    force, wide, node = call(
        lambda *refs: force_kernel(True, *refs),
        "force_first",
        [VMEM] * 6,
        [VMEM] * 3,
        [field_shape, struct(DEPTH - 1, 2, ROWS + 8, NODES), struct(DEPTH, ROWS, NODES)],
    )(disp, masked, row_lo, row_hi, col_lo, col_hi)
    table = pltpu.VMEM((ROWS, 4, NODES), f32)
    tiles = pltpu.VMEM((ROWS, 8, NODES), f32)
    disp, vel, send, surf = call(
        update_kernel,
        "update_first",
        [SMEM] * 3 + [VMEM] * 8,
        [VMEM] * 4,
        [field_shape, field_shape, struct(ENTRIES, 8, NODES), tile_shape],
        [table, tiles, tiles],
    )(scalars(slots), scalars(homes), scalars(rows), returned, reaction, exact, force, disp, vel, mass, surf)

    news = exchange(send)
    low_row, high_row, low_col, high_col, near, exact = call(
        lambda *refs: edge_kernel(False, *refs), "edges_last", [VMEM] * 2, [VMEM] * 6, edge_shapes
    )(disp, surf)
    col_lo = go(high_col, 0, 1)
    col_hi = go(low_col, 0, -1)
    low_out, high_out = call(row_messages, "rows_last", [VMEM] * 4, [VMEM] * 2, [edge_shape] * 2)(
        low_row, high_row, col_lo, col_hi
    )
    row_lo = go(high_out, 1, 0)
    row_hi = go(low_out, -1, 0)
    (total,) = call(contact_last, "contact_last", [SMEM] * 2 + [VMEM] * 4, [VMEM], [tile_shape])(
        scalars(rows), scalars(homes), first, returned, news, near
    )
    disp, vel = call(final_kernel, "update_last", [VMEM] * 11, [VMEM] * 2, [field_shape] * 2, [table])(
        disp, vel, mass, total, exact, wide, node, row_lo, row_hi, col_lo, col_hi
    )
    return disp.transpose(0, 2, 1, 3), vel.transpose(0, 2, 1, 3)


def solution(mesh):
    in_specs = (
        P(None, "gx", None, "gy"),
        P(None, "gx", None, "gy"),
        P("gx", None, "gy"),
        P("gx", None, "gy"),
        P("gx", "gy", None),
    )
    out_specs = (P(None, "gx", None, "gy"), P(None, "gx", None, "gy"))
    return jax.shard_map(local, mesh=mesh, in_specs=in_specs, out_specs=out_specs, check_vma=False)
```

```python
import jax
import jax.numpy as jnp
import numpy as np
from jax import lax
from jax.experimental import pallas as pl
from jax.experimental.pallas import tpu as pltpu
from jax.sharding import PartitionSpec as P

AXES = ("gx", "gy")
NODES = 128
ROWS = 32
DEPTH = 5
FACES = 8
ENTRIES = ROWS * FACES
UNROLL = 128
CHUNKS = 4
LAG = 7

time_step = 0.2
stiff_coef = 4.0 / (8.0 * NODES)
damp_coef = 1.0 / (8.0 * NODES)
exponent_scale = float(np.sqrt(np.log2(np.e) / 2.0))
frame_extent = 4.0

f32 = jnp.float32
bf16 = jnp.bfloat16
PARAMS = pltpu.CompilerParams(vmem_limit_bytes=16 * 1024 * 1024)


def sublanes(shape):
    return lax.broadcasted_iota(jnp.int32, shape, 0)


def lanes(shape):
    return lax.broadcasted_iota(jnp.int32, shape, 1)


def split3(value):
    high = value.astype(bf16).astype(f32)
    rest = value - high
    middle = rest.astype(bf16).astype(f32)
    return high, middle, rest - middle


def frame_tile():
    shape = (8, NODES)
    place = (lanes(shape).astype(f32) - (NODES - 1) / 2.0) * (frame_extent / NODES)
    return jnp.where(sublanes(shape) == 1, place, 0.0)


def tile_constants():
    row = sublanes((8, NODES))
    return frame_tile(), (row < 3).astype(f32), (row == 3).astype(f32), (row == 4).astype(f32)


def tile_parts(disp, vel, consts):
    frame, first3, row3, _ = consts
    place = disp + frame
    scaled = (place * exponent_scale) * first3
    half = 0.5 * jnp.sum(scaled * scaled, axis=0, keepdims=True)
    potential = (stiff_coef * place - damp_coef * vel) * first3 + row3
    return scaled, half, potential


def far_factor(scaled, half, consts):
    h, m, l = split3(scaled + half * consts[2] + consts[3])
    return jnp.concatenate([h, m, h, m, l, h], axis=0).astype(bf16)


def near_factor(scaled, half, consts):
    h, m, l = split3(scaled - consts[2] - half * consts[3])
    return jnp.concatenate([h, h, m, m, h, l], axis=0).astype(bf16)


def packed_potential(potential):
    h, m, l = split3(potential)
    return jnp.concatenate([h + pltpu.roll(m, 4, 0), l], axis=0).astype(bf16)


def fold(total):
    total = total[:8] + total[8:]
    return total + pltpu.roll(total, 4, 0)


def request_kernel(facing_hbm, disp_hbm, vel_hbm, send_ref, slot_ref, home_ref, surf_ref, facing_ref, top_ref, count_ref, sems):
    copies = [
        pltpu.make_async_copy(disp_hbm.at[:, DEPTH - 1], top_ref.at[0], sems.at[0]),
        pltpu.make_async_copy(vel_hbm.at[:, DEPTH - 1], top_ref.at[1], sems.at[1]),
        pltpu.make_async_copy(facing_hbm, facing_ref, sems.at[2]),
    ]
    for copy in copies:
        copy.start()

    def clear(i, carry):
        count_ref[i] = 0
        return carry

    lax.fori_loop(0, NODES, clear, 0, unroll=16)
    for copy in copies:
        copy.wait()
    zero = jnp.zeros((ROWS, NODES), f32)
    for c in range(3):
        surf_ref[:, c, :] = top_ref[0, c]
        surf_ref[:, 3 + c, :] = top_ref[1, c]
        if c < 2:
            surf_ref[:, 6 + c, :] = zero
    row6 = (sublanes((8, NODES)) == 6).astype(f32)

    def visit(b, carry):
        tile = surf_ref[b]
        for k in range(FACES):
            name = facing_ref[k, b]
            block = lax.shift_right_logical(name, 4)
            owner = lax.shift_left(lax.shift_right_logical(block, 5), 4) | (name & 15)
            used = count_ref[owner]
            count_ref[owner] = used + 1
            slot = 2 * owner + used
            slot_ref[b * FACES + k] = slot
            home_ref[slot] = b
            send_ref[slot] = tile + row6 * jnp.full((8, NODES), block & 31, jnp.int32).astype(f32)
        return carry

    lax.fori_loop(0, ROWS, visit, 0, unroll=4)


def near_table(tile, near_ref, b, unit, consts):
    scaled, half, potential = tile_parts(tile, pltpu.roll(tile, 5, 0), consts)
    near = near_factor(scaled, half, consts)
    turned = lax.dot_general(unit, near, (((1,), (1,)), ((), ())), preferred_element_type=f32)
    near_ref[b] = turned.astype(bf16)
    return potential


def unit_matrix():
    shape = (NODES, NODES)
    return (lanes(shape) == sublanes(shape)).astype(bf16)


def table_kernel(surf_ref, near_ref, pot_ref, tail_ref):
    consts = tile_constants()
    unit = unit_matrix()

    def table(b, carry):
        tile = surf_ref[b]
        potential = near_table(tile, near_ref, b, unit, consts)
        pot_ref[b] = packed_potential(potential)
        tail_ref[b] = (pltpu.roll(tile, 3, 0) * consts[2])[:4]
        return carry

    lax.fori_loop(0, ROWS, table, 0, unroll=16)


def edge_kernel(with_stiff, *refs):
    if with_stiff:
        last_ref, disp_ref, surf_ref, stiff_ref, low_row, high_row, low_col, high_col, masked_ref = refs
    else:
        disp_ref, low_row, high_row, low_col, high_col = refs
    shape = (ROWS, NODES)
    lane = lanes(shape)
    if with_stiff:
        row = sublanes(shape)
        keep = ((row < ROWS - 1) | (last_ref[0] == 0)) & ((lane < NODES - 1) | (last_ref[1] == 0))
        for z in range(DEPTH):
            if z < DEPTH - 1:
                masked_ref[z] = jnp.where(keep, stiff_ref[z], 0.0)
            else:
                masked_ref[z] = jnp.zeros(shape, f32)
    low = jnp.zeros(shape, f32)
    high = jnp.zeros(shape, f32)
    low_row[...] = jnp.zeros((24, NODES), f32)
    high_row[...] = jnp.zeros((24, NODES), f32)
    for c in range(4 if with_stiff else 3):
        for z in range(DEPTH):
            at = c * DEPTH + z
            value = disp_ref[c, z] if c < 3 else masked_ref[z]
            low_row[at : at + 1, :] = value[0:1, :]
            high_row[at : at + 1, :] = value[ROWS - 1 :, :]
            low = jnp.where(lane == at, pltpu.roll(value, at, 1) if at else value, low)
            high = jnp.where(lane == at, pltpu.roll(value, at + 1, 1), high)
    low_col[...] = low
    high_col[...] = high


def extended(center, above, below):
    row = sublanes((8, NODES))
    tail = jnp.where(row == 0, below, jnp.where(row == 7, above, 0.0))
    return jnp.concatenate([center, tail], axis=0)


def force_kernel(with_stiff, disp_ref, *refs):
    if with_stiff:
        stiff_ref, row_lo, row_hi, col_lo, col_hi, force_ref, wide_ref, node_ref = refs
    else:
        wide_in, node_in, row_lo, row_hi, col_lo, col_hi, put = refs
    wide = (ROWS + 8, NODES)
    lane = lanes(wide)
    last = lane == NODES - 1
    left = extended(col_lo[...], row_lo[24:25, :], row_hi[24:25, :])
    right = extended(col_hi[...], row_lo[25:26, :], row_hi[25:26, :])

    def own(c, z):
        value = disp_ref[c, z] if c < 3 else stiff_ref[z]
        at = c * DEPTH + z
        return extended(value, row_lo[at : at + 1, :], row_hi[at : at + 1, :])

    def at_last(cols, at):
        return pltpu.roll(cols, NODES - 1 - at, 1)

    def spread(main, side):
        main = main + pltpu.roll(main, 1, 0)
        side = side + pltpu.roll(side, 1, 0)
        return main + pltpu.roll(jnp.where(last, side, main), 1, 1)

    stiff = []
    if with_stiff:
        total = None
        for z in range(DEPTH - 1):
            main = own(3, z)
            side = at_last(left, 3 * DEPTH + z)
            wide_ref[z, 0] = main
            wide_ref[z, 1] = side
            stiff.append((main * 0.125, side * 0.125))
            out = spread(main, side)[:ROWS]
            node_ref[z] = out if total is None else total + out
            total = out
        node_ref[DEPTH - 1] = total
        node = node_ref
    else:
        for z in range(DEPTH - 1):
            stiff.append((wide_in[z, 0] * 0.125, wide_in[z, 1] * 0.125))
        node = node_in
    for c in range(3):
        boxes = []
        for z in range(DEPTH):
            value = own(c, z)
            turned = pltpu.roll(value, NODES - 1, 1)
            main = value + jnp.where(last, at_last(right, c * DEPTH + z), turned)
            side = at_last(left, c * DEPTH + z) + turned
            boxes.append((main, side))
        total = None
        for z in range(DEPTH):
            out = None
            if z < DEPTH - 1:
                main = boxes[z][0] + boxes[z + 1][0]
                side = boxes[z][1] + boxes[z + 1][1]
                main = main + pltpu.roll(main, ROWS + 7, 0)
                side = side + pltpu.roll(side, ROWS + 7, 0)
                out = spread(main * stiff[z][0], side * stiff[z][1])[:ROWS]
                pull = out if total is None else total + out
            else:
                pull = total
            total = out
            force = pull - disp_ref[c, z] * node[z]
            if with_stiff:
                force_ref[c, z] = force
            else:
                put(c, z, force)


def entry_rows(recv_ref, turn_ref, row_ref, sem):
    shape = (NODES, NODES)
    diagonal = lanes(shape) == sublanes(shape)
    for half in range(ENTRIES // NODES):
        held = recv_ref[half * NODES : (half + 1) * NODES, 6, :]
        picked = jnp.sum(jnp.where(diagonal, held, 0.0), axis=0, keepdims=True)
        turn_ref[half : half + 1, :] = picked.astype(jnp.int32)
    copy = pltpu.make_async_copy(turn_ref, row_ref, sem)
    copy.start()
    copy.wait()


def row_messages(low_row, high_row, col_lo, col_hi, low_out, high_out):
    for side, edge, at in ((low_out, low_row, 0), (high_out, high_row, ROWS - 1)):
        side[:24] = edge[...]
        side[24:25] = col_lo[at : at + 1, :]
        side[25:26] = col_hi[at : at + 1, :]
        side[26:] = jnp.zeros((ROWS - 26, NODES), f32)


def pair_loop(row_of, tile_of, near_ref, loc_ref, pot_ref=None, tail_ref=None, out_ref=None):
    consts = tile_constants()

    def visit(step, carry):
        entries = [step * UNROLL + j for j in range(UNROLL)]
        row = [row_of(step, j) for j in range(UNROLL)]
        held = {}

        def weigh(j):
            scaled, half, potential = tile_parts(*tile_of(entries[j]), consts)
            far = far_factor(scaled, half, consts)
            exponent = jnp.dot(near_ref[row[j]], far, preferred_element_type=f32)
            held[j] = exponent, packed_potential(potential), potential

        def reduce(j):
            exponent, far_pot, potential = held[j]
            weight = jnp.exp2(exponent)
            high = weight.astype(bf16)
            low = (weight - high.astype(f32)).astype(bf16)
            pulled = None
            if out_ref is not None:
                near_pot = pot_ref[row[j]]
                pulled = jnp.dot(
                    jnp.concatenate([near_pot, near_pot], axis=1),
                    jnp.concatenate([high, low], axis=0),
                    preferred_element_type=f32,
                )
            pushed = lax.dot_general(
                jnp.concatenate([far_pot, far_pot], axis=1),
                jnp.concatenate([high, low], axis=1),
                (((1,), (1,)), ((), ())),
                preferred_element_type=f32,
            )
            held[j] = pulled, pushed, potential

        def store(j):
            pulled, pushed, potential = held.pop(j)
            if out_ref is not None:
                pulled = fold(pulled)
                out_ref[entries[j]] = (pulled[3:4] * potential - pulled)[:4] + tail_ref[row[j]]
            loc_ref[row[j]] += pushed[:8] + pushed[8:]

        for t in range(UNROLL + LAG + 1):
            if t < UNROLL:
                weigh(t)
            if 0 <= t - LAG < UNROLL:
                reduce(t - LAG)
            if 0 <= t - LAG - 1 < UNROLL:
                store(t - LAG - 1)
        return carry

    lax.fori_loop(0, ENTRIES // UNROLL, visit, 0)


def split_row(row_ref):
    def row_of(step, j):
        first = step * UNROLL
        return row_ref[first // NODES, first % NODES + j]

    return row_of


def wide_tile(value):
    return jnp.concatenate([value, jnp.zeros((4, NODES), f32)], axis=0)


def contact_first(recv_ref, near_ref, pot_ref, tail_ref, low_row, high_row, col_lo, col_hi, *refs):
    out_ref, loc_ref, low_out, high_out, row_ref, turn_ref, sem = refs
    entry_rows(recv_ref, turn_ref, row_ref, sem)
    row_messages(low_row, high_row, col_lo, col_hi, low_out, high_out)
    loc_ref[...] = jnp.zeros((ROWS, 8, NODES), f32)

    def tile_of(e):
        tile = recv_ref[e]
        return tile, pltpu.roll(tile, 5, 0)

    pair_loop(split_row(row_ref), tile_of, near_ref, loc_ref, pot_ref, tail_ref, out_ref)


def contact_last(row_ref, home_ref, first_ref, x_ref, new_ref, disp_ref, vel_ref, loc_ref, near_ref, surf_ref):
    loc_ref[...] = jnp.zeros((ROWS, 8, NODES), f32)
    row = sublanes((8, NODES))
    for c in range(3):
        surf_ref[:, c, :] = disp_ref[c, DEPTH - 1]
        surf_ref[:, 3 + c, :] = vel_ref[c, DEPTH - 1]
        if c < 2:
            surf_ref[:, 6 + c, :] = jnp.zeros((ROWS, NODES), f32)
    consts = tile_constants()
    unit = unit_matrix()
    for b in range(ROWS):
        near_table(surf_ref[b], near_ref, b, unit, consts)

    def faced(e):
        vel = new_ref[e]
        return first_ref[e] + time_step * vel, vel

    def facing(e):
        tile = new_ref[e]
        vel = pltpu.roll(tile, 4, 0)
        x = pltpu.roll(wide_tile(x_ref[e]), 5, 0)
        y = pltpu.roll(tile, 6, 0)
        z = pltpu.roll(tile, 3, 0)
        disp = jnp.where(row == 0, x, jnp.where(row == 1, y, z))
        return disp + time_step * vel, vel

    pair_loop(split_row(row_ref), faced, near_ref, loc_ref)
    pair_loop(lambda step, j: home_ref[step * UNROLL + j], facing, near_ref, loc_ref)


def plane_frame(c):
    if c != 1:
        return 0.0
    shape = (ROWS, NODES)
    return (lanes(shape).astype(f32) - (NODES - 1) / 2.0) * (frame_extent / NODES)


def plane_sum(loc_ref, disp, vel, c):
    weight = loc_ref[:, 3, :] + loc_ref[:, 7, :]
    potential = stiff_coef * (disp + plane_frame(c)) - damp_coef * vel
    return weight * potential - (loc_ref[:, c, :] + loc_ref[:, 4 + c, :])


def update_kernel(slot_ref, home_ref, row_ref, ret_ref, loc_ref, force_ref, disp_ref, vel_ref, mass_ref, *refs):
    new_disp, new_vel, send_hbm, send_ref, surf_ref, sum_ref, facing_tile, faced_tile, sems = refs

    def gather(b, carry):
        acc = ret_ref[slot_ref[b * FACES]]
        for k in range(1, FACES):
            acc = acc + ret_ref[slot_ref[b * FACES + k]]
        sum_ref[b] = acc
        return carry

    lax.fori_loop(0, ROWS, gather, 0, unroll=8)
    last = DEPTH - 1
    mass = time_step * mass_ref[last]
    for c in range(3):
        old, vel = disp_ref[c, last], vel_ref[c, last]
        vel = vel + mass * (force_ref[c, last] + sum_ref[:, c, :] + plane_sum(loc_ref, old, vel, c))
        new_vel[c, last] = vel
        new_disp[c, last] = old + time_step * vel
        surf_ref[:, c, :] = vel
        surf_ref[:, 3 + c, :] = old
    row = sublanes((8, NODES))

    def tiles(b, carry):
        tile = surf_ref[b]
        facing_tile[b] = jnp.where(row < 3, tile, 0.0)
        late = jnp.where(row < 7, pltpu.roll(tile, 4, 0), pltpu.roll(tile, 2, 0))
        faced_tile[b] = jnp.where(row < 3, 0.0, jnp.where(row == 3, pltpu.roll(tile, 7, 0), late))
        return carry

    lax.fori_loop(0, ROWS, tiles, 0, unroll=8)
    size = ENTRIES // CHUNKS
    copies = []
    for chunk in range(CHUNKS):

        def scatter(i, carry, chunk=chunk):
            for j in range(16):
                e = chunk * size + i * 16 + j
                at = (chunk * size) % NODES + i * 16 + j
                r = row_ref[chunk * size // NODES, at]
                send_ref[e] = facing_tile[home_ref[e]] + faced_tile[r]
            return carry

        lax.fori_loop(0, size // 16, scatter, 0)
        part = pl.ds(chunk * size, size)
        copies.append(pltpu.make_async_copy(send_ref.at[part], send_hbm.at[part], sems.at[chunk]))
        copies[-1].start()
    for z in range(DEPTH - 1):
        mass = time_step * mass_ref[z]
        for c in range(3):
            vel = vel_ref[c, z] + mass * force_ref[c, z]
            new_vel[c, z] = vel
            new_disp[c, z] = disp_ref[c, z] + time_step * vel
    for copy in copies:
        copy.wait()


def final_kernel(disp_ref, vel_ref, mass_ref, loc_ref, wide_in, node_in, row_lo, row_hi, col_lo, col_hi, *refs):
    new_disp, new_vel = refs

    def put(c, z, force):
        disp, vel = disp_ref[c, z], vel_ref[c, z]
        if z == DEPTH - 1:
            force = force + plane_sum(loc_ref, disp, vel, c)
        vel = vel + time_step * mass_ref[z] * force
        new_vel[c, z] = vel
        new_disp[c, z] = disp + time_step * vel

    force_kernel(False, disp_ref, wide_in, node_in, row_lo, row_hi, col_lo, col_hi, put)


VMEM = pl.BlockSpec(memory_space=pltpu.VMEM)
SMEM = pl.BlockSpec(memory_space=pltpu.SMEM)
HBM = pl.BlockSpec(memory_space=pltpu.HBM)


def struct(*shape, dtype=f32):
    return jax.ShapeDtypeStruct(shape, dtype)


def shifted(value, count_gx, count_gy, dx, dy):
    pairs = []
    for x in range(count_gx):
        for y in range(count_gy):
            if 0 <= x + dx < count_gx and 0 <= y + dy < count_gy:
                pairs.append((x * count_gy + y, (x + dx) * count_gy + y + dy))
    return lax.ppermute(value, AXES, pairs)


def scalars(value):
    return pltpu.with_memory_space_constraint(value, pltpu.SMEM)


def local(displacement, velocity, stiffness, inverse_mass, facing):
    count_gx = lax.axis_size("gx")
    count_gy = lax.axis_size("gy")
    disp = displacement.transpose(0, 2, 1, 3)
    vel = velocity.transpose(0, 2, 1, 3)
    stiff = stiffness.transpose(1, 0, 2)
    mass = inverse_mass.transpose(1, 0, 2)
    faces = facing.transpose(1, 2, 0).reshape(FACES, ROWS)
    ends = jnp.stack(
        [
            (lax.axis_index("gx") == count_gx - 1).astype(jnp.int32),
            (lax.axis_index("gy") == count_gy - 1).astype(jnp.int32),
        ]
    )
    send, slots, homes, surf = pl.pallas_call(
        request_kernel,
        in_specs=[HBM] * 3,
        out_specs=[VMEM, SMEM, SMEM, VMEM],
        out_shape=[
            struct(ENTRIES, 8, NODES),
            pltpu.SMEM((ENTRIES,), jnp.int32),
            pltpu.SMEM((ENTRIES,), jnp.int32),
            struct(ROWS, 8, NODES),
        ],
        scratch_shapes=[
            pltpu.SMEM((FACES, ROWS), jnp.int32),
            pltpu.VMEM((2, 3, ROWS, NODES), f32),
            pltpu.SMEM((NODES,), jnp.int32),
            pltpu.SemaphoreType.DMA((3,)),
        ],
        compiler_params=PARAMS,
        name="request",
    )(*(pltpu.with_memory_space_constraint(value, pltpu.HBM) for value in (faces, disp, vel)))
    near_shape = struct(ROWS, NODES, 48, dtype=bf16)
    tile_shape = struct(ROWS, 8, NODES)
    small_shape = struct(ROWS, 4, NODES)
    edge_shape = struct(ROWS, NODES)
    edge_shapes = [struct(24, NODES), struct(24, NODES), edge_shape, edge_shape]
    field_shape = struct(3, DEPTH, ROWS, NODES)
    entry_shape = struct(ENTRIES, 4, NODES)

    def go(value, dx, dy):
        return shifted(value, count_gx, count_gy, dx, dy)

    def exchange(value):
        return lax.all_to_all(value, AXES, 0, 0, tiled=True)

    def call(kernel, name, in_specs, out_specs, out_shape, scratch=()):
        return pl.pallas_call(
            kernel,
            in_specs=in_specs,
            out_specs=out_specs,
            out_shape=out_shape,
            scratch_shapes=scratch,
            compiler_params=PARAMS,
            name=name,
        )

    first = exchange(send)
    low_row, high_row, low_col, high_col, masked = call(
        lambda *refs: edge_kernel(True, *refs),
        "edges_first",
        [SMEM] + [VMEM] * 3,
        [VMEM] * 5,
        edge_shapes + [struct(DEPTH, ROWS, NODES)],
    )(ends, disp, surf, stiff)
    col_lo = go(high_col, 0, 1)
    col_hi = go(low_col, 0, -1)
    near, pot, tail = call(
        table_kernel,
        "tables_first",
        [VMEM],
        [VMEM] * 3,
        [near_shape, struct(ROWS, 16, NODES, dtype=bf16), small_shape],
    )(surf)
    action, reaction, low_out, high_out, rows = call(
        contact_first,
        "contact_first",
        [VMEM] * 8,
        [VMEM] * 4 + [SMEM],
        [entry_shape, tile_shape, edge_shape, edge_shape, pltpu.SMEM((ENTRIES // NODES, NODES), jnp.int32)],
        [pltpu.VMEM((ENTRIES // NODES, NODES), jnp.int32), pltpu.SemaphoreType.DMA(())],
    )(first, near, pot, tail, low_row, high_row, col_lo, col_hi)
    returned = exchange(action)
    row_lo = go(high_out, 1, 0)
    row_hi = go(low_out, -1, 0)
    force, wide, node = call(
        lambda *refs: force_kernel(True, *refs),
        "force_first",
        [VMEM] * 6,
        [VMEM] * 3,
        [field_shape, struct(DEPTH - 1, 2, ROWS + 8, NODES), struct(DEPTH, ROWS, NODES)],
    )(disp, masked, row_lo, row_hi, col_lo, col_hi)
    tiles = pltpu.VMEM((ROWS, 8, NODES), f32)
    disp, vel, send = call(
        update_kernel,
        "update_first",
        [SMEM] * 3 + [VMEM] * 6,
        [VMEM] * 2 + [HBM],
        [field_shape, field_shape, pltpu.HBM((ENTRIES, 8, NODES), f32)],
        [
            pltpu.VMEM((ENTRIES, 8, NODES), f32),
            tiles,
            pltpu.VMEM((ROWS, 4, NODES), f32),
            tiles,
            tiles,
            pltpu.SemaphoreType.DMA((CHUNKS,)),
        ],
    )(scalars(slots), scalars(homes), scalars(rows), returned, reaction, force, disp, vel, mass)

    news = exchange(send)
    low_row, high_row, low_col, high_col = call(
        lambda *refs: edge_kernel(False, *refs), "edges_last", [VMEM], [VMEM] * 4, edge_shapes
    )(disp)
    col_lo = go(high_col, 0, 1)
    col_hi = go(low_col, 0, -1)
    low_out, high_out = call(row_messages, "rows_last", [VMEM] * 4, [VMEM] * 2, [edge_shape] * 2)(
        low_row, high_row, col_lo, col_hi
    )
    row_lo = go(high_out, 1, 0)
    row_hi = go(low_out, -1, 0)
    (total,) = call(
        contact_last,
        "contact_last",
        [SMEM] * 2 + [VMEM] * 5,
        [VMEM],
        [tile_shape],
        [pltpu.VMEM((ROWS, NODES, 48), bf16), tiles],
    )(scalars(rows), scalars(homes), first, returned, news, disp, vel)
    disp, vel = call(final_kernel, "update_last", [VMEM] * 10, [VMEM] * 2, [field_shape] * 2)(
        disp, vel, mass, total, wide, node, row_lo, row_hi, col_lo, col_hi
    )
    return disp.transpose(0, 2, 1, 3), vel.transpose(0, 2, 1, 3)


def solution(mesh):
    in_specs = (
        P(None, "gx", None, "gy"),
        P(None, "gx", None, "gy"),
        P("gx", None, "gy"),
        P("gx", None, "gy"),
        P("gx", "gy", None),
    )
    out_specs = (P(None, "gx", None, "gy"), P(None, "gx", None, "gy"))
    return jax.shard_map(local, mesh=mesh, in_specs=in_specs, out_specs=out_specs, check_vma=False)
```

```python
import jax
import jax.numpy as jnp
import numpy as np
from jax import lax
from jax.experimental import pallas as pl
from jax.experimental.pallas import tpu as pltpu
from jax.sharding import PartitionSpec as P

AXES = ("gx", "gy")
NODES = 128
ROWS = 32
DEPTH = 5
FACES = 8
ENTRIES = ROWS * FACES
FIRST_UNROLL = 256
LAST_UNROLL = 128
CHUNKS = 4
LAG = 7

time_step = 0.2
stiff_coef = 4.0 / (8.0 * NODES)
damp_coef = 1.0 / (8.0 * NODES)
exponent_scale = float(np.sqrt(np.log2(np.e) / 2.0))
frame_extent = 4.0

f32 = jnp.float32
bf16 = jnp.bfloat16
PARAMS = pltpu.CompilerParams(vmem_limit_bytes=16 * 1024 * 1024)


def sublanes(shape):
    return lax.broadcasted_iota(jnp.int32, shape, 0)


def lanes(shape):
    return lax.broadcasted_iota(jnp.int32, shape, 1)


def split3(value):
    high = value.astype(bf16).astype(f32)
    rest = value - high
    middle = rest.astype(bf16).astype(f32)
    return high, middle, rest - middle


def frame_tile():
    shape = (8, NODES)
    place = (lanes(shape).astype(f32) - (NODES - 1) / 2.0) * (frame_extent / NODES)
    return jnp.where(sublanes(shape) == 1, place, 0.0)


def tile_constants():
    row = sublanes((8, NODES))
    return frame_tile(), (row < 3).astype(f32), (row == 3).astype(f32), (row == 4).astype(f32)


def tile_parts(disp, vel, consts):
    frame, first3, row3, _ = consts
    place = disp + frame
    scaled = (place * exponent_scale) * first3
    half = 0.5 * jnp.sum(scaled * scaled, axis=0, keepdims=True)
    potential = (stiff_coef * place - damp_coef * vel) * first3 + row3
    return scaled, half, potential


def far_factor(scaled, half, consts):
    h, m, l = split3(scaled + half * consts[2] + consts[3])
    return jnp.concatenate([h, m, h, m, l, h], axis=0).astype(bf16)


def near_factor(scaled, half, consts):
    h, m, l = split3(scaled - consts[2] - half * consts[3])
    return jnp.concatenate([h, h, m, m, h, l], axis=0).astype(bf16)


def packed_potential(potential):
    h, m, l = split3(potential)
    return jnp.concatenate([h + pltpu.roll(m, 4, 0), l], axis=0).astype(bf16)


def fold(total):
    total = total[:8] + total[8:]
    return total + pltpu.roll(total, 4, 0)


def request_kernel(facing_hbm, disp_hbm, vel_hbm, send_ref, slot_ref, home_ref, surf_ref, facing_ref, top_ref, count_ref, sems):
    copies = [
        pltpu.make_async_copy(disp_hbm.at[:, DEPTH - 1], top_ref.at[0], sems.at[0]),
        pltpu.make_async_copy(vel_hbm.at[:, DEPTH - 1], top_ref.at[1], sems.at[1]),
        pltpu.make_async_copy(facing_hbm, facing_ref, sems.at[2]),
    ]
    for copy in copies:
        copy.start()

    def clear(i, carry):
        count_ref[i] = 0
        return carry

    lax.fori_loop(0, NODES, clear, 0, unroll=16)
    for copy in copies:
        copy.wait()
    zero = jnp.zeros((ROWS, NODES), f32)
    for c in range(3):
        surf_ref[:, c, :] = top_ref[0, c]
        surf_ref[:, 3 + c, :] = top_ref[1, c]
        if c < 2:
            surf_ref[:, 6 + c, :] = zero
    row6 = (sublanes((8, NODES)) == 6).astype(f32)

    def visit(b, carry):
        tile = surf_ref[b]
        for k in range(FACES):
            name = facing_ref[k, b]
            block = lax.shift_right_logical(name, 4)
            owner = lax.shift_left(lax.shift_right_logical(block, 5), 4) | (name & 15)
            used = count_ref[owner]
            count_ref[owner] = used + 1
            slot = 2 * owner + used
            slot_ref[b * FACES + k] = slot
            home_ref[slot] = b
            send_ref[slot] = tile + row6 * jnp.full((8, NODES), block & 31, jnp.int32).astype(f32)
        return carry

    lax.fori_loop(0, ROWS, visit, 0, unroll=4)


def near_table(tile, near_ref, b, unit, consts):
    scaled, half, potential = tile_parts(tile, pltpu.roll(tile, 5, 0), consts)
    near = near_factor(scaled, half, consts)
    turned = lax.dot_general(unit, near, (((1,), (1,)), ((), ())), preferred_element_type=f32)
    near_ref[b] = turned.astype(bf16)
    return potential


def unit_matrix():
    shape = (NODES, NODES)
    return (lanes(shape) == sublanes(shape)).astype(bf16)


def table_kernel(surf_ref, near_ref, pot_ref, tail_ref):
    consts = tile_constants()
    unit = unit_matrix()

    def table(b, carry):
        tile = surf_ref[b]
        potential = near_table(tile, near_ref, b, unit, consts)
        pot_ref[b] = packed_potential(potential)
        tail_ref[b] = (pltpu.roll(tile, 3, 0) * consts[2])[:4]
        return carry

    lax.fori_loop(0, ROWS, table, 0, unroll=16)


def edge_kernel(with_stiff, *refs):
    if with_stiff:
        last_ref, disp_ref, surf_ref, stiff_ref, low_row, high_row, low_col, high_col, masked_ref = refs
    else:
        disp_ref, low_row, high_row, low_col, high_col = refs
    shape = (ROWS, NODES)
    lane = lanes(shape)
    if with_stiff:
        row = sublanes(shape)
        keep = ((row < ROWS - 1) | (last_ref[0] == 0)) & ((lane < NODES - 1) | (last_ref[1] == 0))
        for z in range(DEPTH):
            if z < DEPTH - 1:
                masked_ref[z] = jnp.where(keep, stiff_ref[z], 0.0)
            else:
                masked_ref[z] = jnp.zeros(shape, f32)
    low = jnp.zeros(shape, f32)
    high = jnp.zeros(shape, f32)
    low_row[...] = jnp.zeros((24, NODES), f32)
    high_row[...] = jnp.zeros((24, NODES), f32)
    for c in range(4 if with_stiff else 3):
        for z in range(DEPTH):
            at = c * DEPTH + z
            value = disp_ref[c, z] if c < 3 else masked_ref[z]
            low_row[at : at + 1, :] = value[0:1, :]
            high_row[at : at + 1, :] = value[ROWS - 1 :, :]
            low = jnp.where(lane == at, pltpu.roll(value, at, 1) if at else value, low)
            high = jnp.where(lane == at, pltpu.roll(value, at + 1, 1), high)
    low_col[...] = low
    high_col[...] = high


def extended(center, above, below):
    row = sublanes((8, NODES))
    tail = jnp.where(row == 0, below, jnp.where(row == 7, above, 0.0))
    return jnp.concatenate([center, tail], axis=0)


def force_kernel(with_stiff, disp_ref, *refs):
    if with_stiff:
        stiff_ref, row_lo, row_hi, col_lo, col_hi, force_ref, wide_ref, node_ref = refs
    else:
        wide_in, node_in, row_lo, row_hi, col_lo, col_hi, put = refs
    wide = (ROWS + 8, NODES)
    lane = lanes(wide)
    last = lane == NODES - 1
    left = extended(col_lo[...], row_lo[24:25, :], row_hi[24:25, :])
    right = extended(col_hi[...], row_lo[25:26, :], row_hi[25:26, :])

    def own(c, z):
        value = disp_ref[c, z] if c < 3 else stiff_ref[z]
        at = c * DEPTH + z
        return extended(value, row_lo[at : at + 1, :], row_hi[at : at + 1, :])

    def at_last(cols, at):
        return pltpu.roll(cols, NODES - 1 - at, 1)

    def spread(main, side):
        main = main + pltpu.roll(main, 1, 0)
        side = side + pltpu.roll(side, 1, 0)
        return main + pltpu.roll(jnp.where(last, side, main), 1, 1)

    stiff = []
    if with_stiff:
        total = None
        for z in range(DEPTH - 1):
            main = own(3, z)
            side = at_last(left, 3 * DEPTH + z)
            wide_ref[z, 0] = main
            wide_ref[z, 1] = side
            stiff.append((main * 0.125, side * 0.125))
            out = spread(main, side)[:ROWS]
            node_ref[z] = out if total is None else total + out
            total = out
        node_ref[DEPTH - 1] = total
        node = node_ref
    else:
        for z in range(DEPTH - 1):
            stiff.append((wide_in[z, 0] * 0.125, wide_in[z, 1] * 0.125))
        node = node_in
    for c in range(3):
        boxes = []
        for z in range(DEPTH):
            value = own(c, z)
            turned = pltpu.roll(value, NODES - 1, 1)
            main = value + jnp.where(last, at_last(right, c * DEPTH + z), turned)
            side = at_last(left, c * DEPTH + z) + turned
            boxes.append((main, side))
        total = None
        for z in range(DEPTH):
            out = None
            if z < DEPTH - 1:
                main = boxes[z][0] + boxes[z + 1][0]
                side = boxes[z][1] + boxes[z + 1][1]
                main = main + pltpu.roll(main, ROWS + 7, 0)
                side = side + pltpu.roll(side, ROWS + 7, 0)
                out = spread(main * stiff[z][0], side * stiff[z][1])[:ROWS]
                pull = out if total is None else total + out
            else:
                pull = total
            total = out
            force = pull - disp_ref[c, z] * node[z]
            if with_stiff:
                force_ref[c, z] = force
            else:
                put(c, z, force)


def entry_rows(recv_ref, turn_ref, row_ref, sem):
    shape = (NODES, NODES)
    diagonal = lanes(shape) == sublanes(shape)
    for half in range(ENTRIES // NODES):
        held = recv_ref[half * NODES : (half + 1) * NODES, 6, :]
        picked = jnp.sum(jnp.where(diagonal, held, 0.0), axis=0, keepdims=True)
        turn_ref[half : half + 1, :] = picked.astype(jnp.int32)
    copy = pltpu.make_async_copy(turn_ref, row_ref, sem)
    copy.start()
    copy.wait()


def row_messages(low_row, high_row, col_lo, col_hi, low_out, high_out):
    for side, edge, at in ((low_out, low_row, 0), (high_out, high_row, ROWS - 1)):
        side[:24] = edge[...]
        side[24:25] = col_lo[at : at + 1, :]
        side[25:26] = col_hi[at : at + 1, :]
        side[26:] = jnp.zeros((ROWS - 26, NODES), f32)


def pair_loop(unroll, row_of, tile_of, near_ref, loc_ref, pot_ref=None, tail_ref=None, out_ref=None):
    consts = tile_constants()

    def visit(step, carry):
        entries = [step * unroll + j for j in range(unroll)]
        row = [row_of(step, j) for j in range(unroll)]
        held = {}

        def weigh(j):
            scaled, half, potential = tile_parts(*tile_of(entries[j]), consts)
            far = far_factor(scaled, half, consts)
            exponent = jnp.dot(near_ref[row[j]], far, preferred_element_type=f32)
            held[j] = exponent, packed_potential(potential), potential

        def reduce(j):
            exponent, far_pot, potential = held[j]
            weight = jnp.exp2(exponent)
            high = weight.astype(bf16)
            low = (weight - high.astype(f32)).astype(bf16)
            pulled = None
            if out_ref is not None:
                near_pot = pot_ref[row[j]]
                pulled = jnp.dot(
                    jnp.concatenate([near_pot, near_pot], axis=1),
                    jnp.concatenate([high, low], axis=0),
                    preferred_element_type=f32,
                )
            pushed = lax.dot_general(
                jnp.concatenate([far_pot, far_pot], axis=1),
                jnp.concatenate([high, low], axis=1),
                (((1,), (1,)), ((), ())),
                preferred_element_type=f32,
            )
            held[j] = pulled, pushed, potential

        def store(j):
            pulled, pushed, potential = held.pop(j)
            if out_ref is not None:
                pulled = fold(pulled)
                out_ref[entries[j]] = (pulled[3:4] * potential - pulled)[:4] + tail_ref[row[j]]
            loc_ref[row[j]] += pushed[:8] + pushed[8:]

        for t in range(unroll + LAG + 1):
            if t < unroll:
                weigh(t)
            if 0 <= t - LAG < unroll:
                reduce(t - LAG)
            if 0 <= t - LAG - 1 < unroll:
                store(t - LAG - 1)
        return carry

    lax.fori_loop(0, ENTRIES // unroll, visit, 0)


def split_row(unroll, row_ref):
    def row_of(step, j):
        if unroll >= NODES:
            return row_ref[step * (unroll // NODES) + j // NODES, j % NODES]
        first = step * unroll
        return row_ref[first // NODES, first % NODES + j]

    return row_of


def wide_tile(value):
    return jnp.concatenate([value, jnp.zeros((4, NODES), f32)], axis=0)


def contact_first(recv_ref, near_ref, pot_ref, tail_ref, low_row, high_row, col_lo, col_hi, *refs):
    out_ref, loc_ref, low_out, high_out, row_ref, turn_ref, sem = refs
    entry_rows(recv_ref, turn_ref, row_ref, sem)
    row_messages(low_row, high_row, col_lo, col_hi, low_out, high_out)
    loc_ref[...] = jnp.zeros((ROWS, 8, NODES), f32)

    def tile_of(e):
        tile = recv_ref[e]
        return tile, pltpu.roll(tile, 5, 0)

    pair_loop(FIRST_UNROLL, split_row(FIRST_UNROLL, row_ref), tile_of, near_ref, loc_ref, pot_ref, tail_ref, out_ref)


def contact_last(row_ref, home_ref, first_ref, x_ref, new_ref, disp_ref, vel_ref, loc_ref, near_ref, surf_ref):
    loc_ref[...] = jnp.zeros((ROWS, 8, NODES), f32)
    row = sublanes((8, NODES))
    for c in range(3):
        surf_ref[:, c, :] = disp_ref[c, DEPTH - 1]
        surf_ref[:, 3 + c, :] = vel_ref[c, DEPTH - 1]
        if c < 2:
            surf_ref[:, 6 + c, :] = jnp.zeros((ROWS, NODES), f32)
    consts = tile_constants()
    unit = unit_matrix()
    for b in range(ROWS):
        near_table(surf_ref[b], near_ref, b, unit, consts)

    def faced(e):
        vel = new_ref[e]
        return first_ref[e] + time_step * vel, vel

    def facing(e):
        tile = new_ref[e]
        vel = pltpu.roll(tile, 4, 0)
        x = pltpu.roll(wide_tile(x_ref[e]), 5, 0)
        y = pltpu.roll(tile, 6, 0)
        z = pltpu.roll(tile, 3, 0)
        disp = jnp.where(row == 0, x, jnp.where(row == 1, y, z))
        return disp + time_step * vel, vel

    pair_loop(LAST_UNROLL, split_row(LAST_UNROLL, row_ref), faced, near_ref, loc_ref)
    pair_loop(LAST_UNROLL, lambda step, j: home_ref[step * LAST_UNROLL + j], facing, near_ref, loc_ref)


def plane_frame(c):
    if c != 1:
        return 0.0
    shape = (ROWS, NODES)
    return (lanes(shape).astype(f32) - (NODES - 1) / 2.0) * (frame_extent / NODES)


def plane_sum(loc_ref, disp, vel, c):
    weight = loc_ref[:, 3, :] + loc_ref[:, 7, :]
    potential = stiff_coef * (disp + plane_frame(c)) - damp_coef * vel
    return weight * potential - (loc_ref[:, c, :] + loc_ref[:, 4 + c, :])


def update_kernel(slot_ref, home_ref, row_ref, ret_ref, loc_ref, force_ref, disp_ref, vel_ref, mass_ref, *refs):
    new_disp, new_vel, send_hbm, send_ref, surf_ref, sum_ref, facing_tile, faced_tile, sems = refs

    def gather(b, carry):
        acc = ret_ref[slot_ref[b * FACES]]
        for k in range(1, FACES):
            acc = acc + ret_ref[slot_ref[b * FACES + k]]
        sum_ref[b] = acc
        return carry

    lax.fori_loop(0, ROWS, gather, 0, unroll=8)
    last = DEPTH - 1
    mass = time_step * mass_ref[last]
    for c in range(3):
        old, vel = disp_ref[c, last], vel_ref[c, last]
        vel = vel + mass * (force_ref[c, last] + sum_ref[:, c, :] + plane_sum(loc_ref, old, vel, c))
        new_vel[c, last] = vel
        new_disp[c, last] = old + time_step * vel
        surf_ref[:, c, :] = vel
        surf_ref[:, 3 + c, :] = old
    row = sublanes((8, NODES))

    def tiles(b, carry):
        tile = surf_ref[b]
        facing_tile[b] = jnp.where(row < 3, tile, 0.0)
        late = jnp.where(row < 7, pltpu.roll(tile, 4, 0), pltpu.roll(tile, 2, 0))
        faced_tile[b] = jnp.where(row < 3, 0.0, jnp.where(row == 3, pltpu.roll(tile, 7, 0), late))
        return carry

    lax.fori_loop(0, ROWS, tiles, 0, unroll=8)
    size = ENTRIES // CHUNKS
    copies = []
    for chunk in range(CHUNKS):

        def scatter(i, carry, chunk=chunk):
            for j in range(16):
                e = chunk * size + i * 16 + j
                at = (chunk * size) % NODES + i * 16 + j
                r = row_ref[chunk * size // NODES, at]
                send_ref[e] = facing_tile[home_ref[e]] + faced_tile[r]
            return carry

        lax.fori_loop(0, size // 16, scatter, 0)
        part = pl.ds(chunk * size, size)
        copies.append(pltpu.make_async_copy(send_ref.at[part], send_hbm.at[part], sems.at[chunk]))
        copies[-1].start()
    for z in range(DEPTH - 1):
        mass = time_step * mass_ref[z]
        for c in range(3):
            vel = vel_ref[c, z] + mass * force_ref[c, z]
            new_vel[c, z] = vel
            new_disp[c, z] = disp_ref[c, z] + time_step * vel
    for copy in copies:
        copy.wait()


def final_kernel(disp_ref, vel_ref, mass_ref, loc_ref, wide_in, node_in, row_lo, row_hi, col_lo, col_hi, *refs):
    new_disp, new_vel = refs

    def put(c, z, force):
        disp, vel = disp_ref[c, z], vel_ref[c, z]
        if z == DEPTH - 1:
            force = force + plane_sum(loc_ref, disp, vel, c)
        vel = vel + time_step * mass_ref[z] * force
        new_vel[c, z] = vel
        new_disp[c, z] = disp + time_step * vel

    force_kernel(False, disp_ref, wide_in, node_in, row_lo, row_hi, col_lo, col_hi, put)


VMEM = pl.BlockSpec(memory_space=pltpu.VMEM)
SMEM = pl.BlockSpec(memory_space=pltpu.SMEM)
HBM = pl.BlockSpec(memory_space=pltpu.HBM)


def struct(*shape, dtype=f32):
    return jax.ShapeDtypeStruct(shape, dtype)


def shifted(value, count_gx, count_gy, dx, dy):
    pairs = []
    for x in range(count_gx):
        for y in range(count_gy):
            if 0 <= x + dx < count_gx and 0 <= y + dy < count_gy:
                pairs.append((x * count_gy + y, (x + dx) * count_gy + y + dy))
    return lax.ppermute(value, AXES, pairs)


def scalars(value):
    return pltpu.with_memory_space_constraint(value, pltpu.SMEM)


def local(displacement, velocity, stiffness, inverse_mass, facing):
    count_gx = lax.axis_size("gx")
    count_gy = lax.axis_size("gy")
    disp = displacement.transpose(0, 2, 1, 3)
    vel = velocity.transpose(0, 2, 1, 3)
    stiff = stiffness.transpose(1, 0, 2)
    mass = inverse_mass.transpose(1, 0, 2)
    faces = facing.transpose(1, 2, 0).reshape(FACES, ROWS)
    ends = jnp.stack(
        [
            (lax.axis_index("gx") == count_gx - 1).astype(jnp.int32),
            (lax.axis_index("gy") == count_gy - 1).astype(jnp.int32),
        ]
    )
    send, slots, homes, surf = pl.pallas_call(
        request_kernel,
        in_specs=[HBM] * 3,
        out_specs=[VMEM, SMEM, SMEM, VMEM],
        out_shape=[
            struct(ENTRIES, 8, NODES),
            pltpu.SMEM((ENTRIES,), jnp.int32),
            pltpu.SMEM((ENTRIES,), jnp.int32),
            struct(ROWS, 8, NODES),
        ],
        scratch_shapes=[
            pltpu.SMEM((FACES, ROWS), jnp.int32),
            pltpu.VMEM((2, 3, ROWS, NODES), f32),
            pltpu.SMEM((NODES,), jnp.int32),
            pltpu.SemaphoreType.DMA((3,)),
        ],
        compiler_params=PARAMS,
        name="request",
    )(*(pltpu.with_memory_space_constraint(value, pltpu.HBM) for value in (faces, disp, vel)))
    near_shape = struct(ROWS, NODES, 48, dtype=bf16)
    tile_shape = struct(ROWS, 8, NODES)
    small_shape = struct(ROWS, 4, NODES)
    edge_shape = struct(ROWS, NODES)
    edge_shapes = [struct(24, NODES), struct(24, NODES), edge_shape, edge_shape]
    field_shape = struct(3, DEPTH, ROWS, NODES)
    entry_shape = struct(ENTRIES, 4, NODES)

    def go(value, dx, dy):
        return shifted(value, count_gx, count_gy, dx, dy)

    def exchange(value):
        return lax.all_to_all(value, AXES, 0, 0, tiled=True)

    def call(kernel, name, in_specs, out_specs, out_shape, scratch=()):
        return pl.pallas_call(
            kernel,
            in_specs=in_specs,
            out_specs=out_specs,
            out_shape=out_shape,
            scratch_shapes=scratch,
            compiler_params=PARAMS,
            name=name,
        )

    first = exchange(send)
    low_row, high_row, low_col, high_col, masked = call(
        lambda *refs: edge_kernel(True, *refs),
        "edges_first",
        [SMEM] + [VMEM] * 3,
        [VMEM] * 5,
        edge_shapes + [struct(DEPTH, ROWS, NODES)],
    )(ends, disp, surf, stiff)
    col_lo = go(high_col, 0, 1)
    col_hi = go(low_col, 0, -1)
    near, pot, tail = call(
        table_kernel,
        "tables_first",
        [VMEM],
        [VMEM] * 3,
        [near_shape, struct(ROWS, 16, NODES, dtype=bf16), small_shape],
    )(surf)
    action, reaction, low_out, high_out, rows = call(
        contact_first,
        "contact_first",
        [VMEM] * 8,
        [VMEM] * 4 + [SMEM],
        [entry_shape, tile_shape, edge_shape, edge_shape, pltpu.SMEM((ENTRIES // NODES, NODES), jnp.int32)],
        [pltpu.VMEM((ENTRIES // NODES, NODES), jnp.int32), pltpu.SemaphoreType.DMA(())],
    )(first, near, pot, tail, low_row, high_row, col_lo, col_hi)
    returned = exchange(action)
    row_lo = go(high_out, 1, 0)
    row_hi = go(low_out, -1, 0)
    force, wide, node = call(
        lambda *refs: force_kernel(True, *refs),
        "force_first",
        [VMEM] * 6,
        [VMEM] * 3,
        [field_shape, struct(DEPTH - 1, 2, ROWS + 8, NODES), struct(DEPTH, ROWS, NODES)],
    )(disp, masked, row_lo, row_hi, col_lo, col_hi)
    tiles = pltpu.VMEM((ROWS, 8, NODES), f32)
    disp, vel, send = call(
        update_kernel,
        "update_first",
        [SMEM] * 3 + [VMEM] * 6,
        [VMEM] * 2 + [HBM],
        [field_shape, field_shape, pltpu.HBM((ENTRIES, 8, NODES), f32)],
        [
            pltpu.VMEM((ENTRIES, 8, NODES), f32),
            tiles,
            pltpu.VMEM((ROWS, 4, NODES), f32),
            tiles,
            tiles,
            pltpu.SemaphoreType.DMA((CHUNKS,)),
        ],
    )(scalars(slots), scalars(homes), scalars(rows), returned, reaction, force, disp, vel, mass)

    news = exchange(send)
    low_row, high_row, low_col, high_col = call(
        lambda *refs: edge_kernel(False, *refs), "edges_last", [VMEM], [VMEM] * 4, edge_shapes
    )(disp)
    col_lo = go(high_col, 0, 1)
    col_hi = go(low_col, 0, -1)
    low_out, high_out = call(row_messages, "rows_last", [VMEM] * 4, [VMEM] * 2, [edge_shape] * 2)(
        low_row, high_row, col_lo, col_hi
    )
    row_lo = go(high_out, 1, 0)
    row_hi = go(low_out, -1, 0)
    (total,) = call(
        contact_last,
        "contact_last",
        [SMEM] * 2 + [VMEM] * 5,
        [VMEM],
        [tile_shape],
        [pltpu.VMEM((ROWS, NODES, 48), bf16), tiles],
    )(scalars(rows), scalars(homes), first, returned, news, disp, vel)
    disp, vel = call(final_kernel, "update_last", [VMEM] * 10, [VMEM] * 2, [field_shape] * 2)(
        disp, vel, mass, total, wide, node, row_lo, row_hi, col_lo, col_hi
    )
    return disp.transpose(0, 2, 1, 3), vel.transpose(0, 2, 1, 3)


def solution(mesh):
    in_specs = (
        P(None, "gx", None, "gy"),
        P(None, "gx", None, "gy"),
        P("gx", None, "gy"),
        P("gx", None, "gy"),
        P("gx", "gy", None),
    )
    out_specs = (P(None, "gx", None, "gy"), P(None, "gx", None, "gy"))
    return jax.shard_map(local, mesh=mesh, in_specs=in_specs, out_specs=out_specs, check_vma=False)
```

```python
import jax
import jax.numpy as jnp
import numpy as np
from jax import lax
from jax.experimental import pallas as pl
from jax.experimental.pallas import tpu as pltpu
from jax.sharding import PartitionSpec as P

AXES = ("gx", "gy")
NODES = 128
ROWS = 32
DEPTH = 5
FACES = 8
ENTRIES = ROWS * FACES
FIRST_UNROLL = 256
LAST_UNROLL = 128
CHUNKS = 4
LAG = 7

time_step = 0.2
stiff_coef = 4.0 / (8.0 * NODES)
damp_coef = 1.0 / (8.0 * NODES)
exponent_scale = float(np.sqrt(np.log2(np.e) / 2.0))
frame_extent = 4.0

f32 = jnp.float32
bf16 = jnp.bfloat16
PARAMS = pltpu.CompilerParams(vmem_limit_bytes=16 * 1024 * 1024)


def sublanes(shape):
    return lax.broadcasted_iota(jnp.int32, shape, 0)


def lanes(shape):
    return lax.broadcasted_iota(jnp.int32, shape, 1)


def split3(value):
    high = value.astype(bf16).astype(f32)
    rest = value - high
    middle = rest.astype(bf16).astype(f32)
    return high, middle, rest - middle


def frame_tile():
    shape = (8, NODES)
    place = (lanes(shape).astype(f32) - (NODES - 1) / 2.0) * (frame_extent / NODES)
    return jnp.where(sublanes(shape) == 1, place, 0.0)


def tile_constants():
    row = sublanes((8, NODES))
    return frame_tile(), (row < 3).astype(f32), (row == 3).astype(f32), (row == 4).astype(f32)


def tile_parts(disp, vel, consts):
    frame, first3, row3, _ = consts
    place = disp + frame
    scaled = (place * exponent_scale) * first3
    half = 0.5 * jnp.sum(scaled * scaled, axis=0, keepdims=True)
    potential = (stiff_coef * place - damp_coef * vel) * first3 + row3
    return scaled, half, potential


def far_factor(scaled, half, consts):
    h, m, l = split3(scaled + half * consts[2] + consts[3])
    return jnp.concatenate([h, m, h, m, l, h], axis=0).astype(bf16)


def near_factor(scaled, half, consts):
    h, m, l = split3(scaled - consts[2] - half * consts[3])
    return jnp.concatenate([h, h, m, m, h, l], axis=0).astype(bf16)


def packed_potential(potential):
    h, m, l = split3(potential)
    return jnp.concatenate([h + pltpu.roll(m, 4, 0), l], axis=0).astype(bf16)


def fold(total):
    total = total[:8] + total[8:]
    return total + pltpu.roll(total, 4, 0)


def request_kernel(facing_hbm, disp_hbm, vel_hbm, send_ref, slot_ref, home_ref, surf_ref, facing_ref, top_ref, count_ref, sems):
    copies = [
        pltpu.make_async_copy(disp_hbm.at[:, DEPTH - 1], top_ref.at[0], sems.at[0]),
        pltpu.make_async_copy(vel_hbm.at[:, DEPTH - 1], top_ref.at[1], sems.at[1]),
        pltpu.make_async_copy(facing_hbm, facing_ref, sems.at[2]),
    ]
    for copy in copies:
        copy.start()

    def clear(i, carry):
        count_ref[i] = 0
        return carry

    lax.fori_loop(0, NODES, clear, 0, unroll=16)
    for copy in copies:
        copy.wait()
    zero = jnp.zeros((ROWS, NODES), f32)
    for c in range(3):
        surf_ref[:, c, :] = top_ref[0, c]
        surf_ref[:, 3 + c, :] = top_ref[1, c]
        if c < 2:
            surf_ref[:, 6 + c, :] = zero
    row6 = (sublanes((8, NODES)) == 6).astype(f32)

    def visit(b, carry):
        tile = surf_ref[b]
        for k in range(FACES):
            name = facing_ref[k, b]
            block = lax.shift_right_logical(name, 4)
            owner = lax.shift_left(lax.shift_right_logical(block, 5), 4) | (name & 15)
            used = count_ref[owner]
            count_ref[owner] = used + 1
            slot = 2 * owner + used
            slot_ref[b * FACES + k] = slot
            home_ref[slot] = b
            send_ref[slot] = tile + row6 * jnp.full((8, NODES), block & 31, jnp.int32).astype(f32)
        return carry

    lax.fori_loop(0, ROWS, visit, 0, unroll=4)


def near_table(tile, near_ref, b, unit, consts):
    scaled, half, potential = tile_parts(tile, pltpu.roll(tile, 5, 0), consts)
    near = near_factor(scaled, half, consts)
    turned = lax.dot_general(unit, near, (((1,), (1,)), ((), ())), preferred_element_type=f32)
    near_ref[b] = turned.astype(bf16)
    return potential


def unit_matrix():
    shape = (NODES, NODES)
    return (lanes(shape) == sublanes(shape)).astype(bf16)


def table_kernel(surf_ref, near_ref, pot_ref, tail_ref):
    consts = tile_constants()
    unit = unit_matrix()

    def table(b, carry):
        tile = surf_ref[b]
        potential = near_table(tile, near_ref, b, unit, consts)
        pot_ref[b] = packed_potential(potential)
        tail_ref[b] = (pltpu.roll(tile, 3, 0) * consts[2])[:4]
        return carry

    lax.fori_loop(0, ROWS, table, 0, unroll=16)


def edge_kernel(with_stiff, *refs):
    if with_stiff:
        last_ref, disp_ref, surf_ref, stiff_ref, low_row, high_row, low_col, high_col, masked_ref = refs
    else:
        disp_ref, low_row, high_row, low_col, high_col = refs
    shape = (ROWS, NODES)
    lane = lanes(shape)
    if with_stiff:
        row = sublanes(shape)
        keep = ((row < ROWS - 1) | (last_ref[0] == 0)) & ((lane < NODES - 1) | (last_ref[1] == 0))
        for z in range(DEPTH):
            if z < DEPTH - 1:
                masked_ref[z] = jnp.where(keep, stiff_ref[z], 0.0)
            else:
                masked_ref[z] = jnp.zeros(shape, f32)
    low = jnp.zeros(shape, f32)
    high = jnp.zeros(shape, f32)
    low_row[...] = jnp.zeros((24, NODES), f32)
    high_row[...] = jnp.zeros((24, NODES), f32)
    for c in range(4 if with_stiff else 3):
        for z in range(DEPTH):
            at = c * DEPTH + z
            value = disp_ref[c, z] if c < 3 else masked_ref[z]
            low_row[at : at + 1, :] = value[0:1, :]
            high_row[at : at + 1, :] = value[ROWS - 1 :, :]
            low = jnp.where(lane == at, pltpu.roll(value, at, 1) if at else value, low)
            high = jnp.where(lane == at, pltpu.roll(value, at + 1, 1), high)
    low_col[...] = low
    high_col[...] = high


def extended(center, above, below):
    row = sublanes((8, NODES))
    tail = jnp.where(row == 0, below, jnp.where(row == 7, above, 0.0))
    return jnp.concatenate([center, tail], axis=0)


def force_kernel(with_stiff, disp_ref, *refs):
    if with_stiff:
        stiff_ref, row_lo, row_hi, col_lo, col_hi, force_ref, wide_ref, node_ref = refs
    else:
        wide_in, node_in, row_lo, row_hi, col_lo, col_hi, put = refs
    wide = (ROWS + 8, NODES)
    lane = lanes(wide)
    last = lane == NODES - 1
    left = extended(col_lo[...], row_lo[24:25, :], row_hi[24:25, :])
    right = extended(col_hi[...], row_lo[25:26, :], row_hi[25:26, :])

    def own(c, z):
        value = disp_ref[c, z] if c < 3 else stiff_ref[z]
        at = c * DEPTH + z
        return extended(value, row_lo[at : at + 1, :], row_hi[at : at + 1, :])

    def at_last(cols, at):
        return pltpu.roll(cols, NODES - 1 - at, 1)

    def spread(main, side):
        main = main + pltpu.roll(main, 1, 0)
        side = side + pltpu.roll(side, 1, 0)
        return main + pltpu.roll(jnp.where(last, side, main), 1, 1)

    stiff = []
    if with_stiff:
        total = None
        for z in range(DEPTH - 1):
            main = own(3, z)
            side = at_last(left, 3 * DEPTH + z)
            wide_ref[z, 0] = main
            wide_ref[z, 1] = side
            stiff.append((main * 0.125, side * 0.125))
            out = spread(main, side)[:ROWS]
            node_ref[z] = out if total is None else total + out
            total = out
        node_ref[DEPTH - 1] = total
        node = node_ref
    else:
        for z in range(DEPTH - 1):
            stiff.append((wide_in[z, 0] * 0.125, wide_in[z, 1] * 0.125))
        node = node_in
    for c in range(3):
        boxes = []
        for z in range(DEPTH):
            value = own(c, z)
            turned = pltpu.roll(value, NODES - 1, 1)
            main = value + jnp.where(last, at_last(right, c * DEPTH + z), turned)
            side = at_last(left, c * DEPTH + z) + turned
            boxes.append((main, side))
        total = None
        for z in range(DEPTH):
            out = None
            if z < DEPTH - 1:
                main = boxes[z][0] + boxes[z + 1][0]
                side = boxes[z][1] + boxes[z + 1][1]
                main = main + pltpu.roll(main, ROWS + 7, 0)
                side = side + pltpu.roll(side, ROWS + 7, 0)
                out = spread(main * stiff[z][0], side * stiff[z][1])[:ROWS]
                pull = out if total is None else total + out
            else:
                pull = total
            total = out
            force = pull - disp_ref[c, z] * node[z]
            if with_stiff:
                force_ref[c, z] = force
            else:
                put(c, z, force)


def entry_rows(recv_ref, turn_ref, row_ref, sem):
    shape = (NODES, NODES)
    diagonal = lanes(shape) == sublanes(shape)
    for half in range(ENTRIES // NODES):
        held = recv_ref[half * NODES : (half + 1) * NODES, 6, :]
        picked = jnp.sum(jnp.where(diagonal, held, 0.0), axis=0, keepdims=True)
        turn_ref[half : half + 1, :] = picked.astype(jnp.int32)
    copy = pltpu.make_async_copy(turn_ref, row_ref, sem)
    copy.start()
    copy.wait()


def row_messages(low_row, high_row, col_lo, col_hi, low_out, high_out):
    for side, edge, at in ((low_out, low_row, 0), (high_out, high_row, ROWS - 1)):
        side[:24] = edge[...]
        side[24:25] = col_lo[at : at + 1, :]
        side[25:26] = col_hi[at : at + 1, :]
        side[26:] = jnp.zeros((ROWS - 26, NODES), f32)


def pair_loop(steps, unroll, row_of, tile_of, near_ref, loc_ref, pot_ref=None, tail_ref=None, out_ref=None):
    consts = tile_constants()

    def visit(step, carry):
        entries = [step * unroll + j for j in range(unroll)]
        row = [row_of(step, j) for j in range(unroll)]
        held = {}

        def weigh(j):
            scaled, half, potential = tile_parts(*tile_of(step, j), consts)
            far = far_factor(scaled, half, consts)
            exponent = jnp.dot(near_ref[row[j]], far, preferred_element_type=f32)
            held[j] = exponent, packed_potential(potential), potential

        def reduce(j):
            exponent, far_pot, potential = held[j]
            weight = jnp.exp2(exponent)
            high = weight.astype(bf16)
            low = (weight - high.astype(f32)).astype(bf16)
            pulled = None
            if out_ref is not None:
                near_pot = pot_ref[row[j]]
                pulled = jnp.dot(
                    jnp.concatenate([near_pot, near_pot], axis=1),
                    jnp.concatenate([high, low], axis=0),
                    preferred_element_type=f32,
                )
            pushed = lax.dot_general(
                jnp.concatenate([far_pot, far_pot], axis=1),
                jnp.concatenate([high, low], axis=1),
                (((1,), (1,)), ((), ())),
                preferred_element_type=f32,
            )
            held[j] = pulled, pushed, potential

        def store(j):
            pulled, pushed, potential = held.pop(j)
            if out_ref is not None:
                pulled = fold(pulled)
                out_ref[entries[j]] = (pulled[3:4] * potential - pulled)[:4] + tail_ref[row[j]]
            loc_ref[row[j]] += pushed[:8] + pushed[8:]

        for t in range(unroll + LAG + 1):
            if t < unroll:
                weigh(t)
            if 0 <= t - LAG < unroll:
                reduce(t - LAG)
            if 0 <= t - LAG - 1 < unroll:
                store(t - LAG - 1)
        return carry

    lax.fori_loop(0, steps, visit, 0)


def split_row(unroll, row_ref):
    def row_of(step, j):
        if unroll >= NODES:
            return row_ref[step * (unroll // NODES) + j // NODES, j % NODES]
        first = step * unroll
        return row_ref[first // NODES, first % NODES + j]

    return row_of


def wide_tile(value):
    return jnp.concatenate([value, jnp.zeros((4, NODES), f32)], axis=0)


def contact_first(recv_ref, near_ref, pot_ref, tail_ref, low_row, high_row, col_lo, col_hi, *refs):
    out_ref, loc_ref, low_out, high_out, row_ref, turn_ref, sem = refs
    entry_rows(recv_ref, turn_ref, row_ref, sem)
    row_messages(low_row, high_row, col_lo, col_hi, low_out, high_out)
    loc_ref[...] = jnp.zeros((ROWS, 8, NODES), f32)

    def tile_of(step, j):
        tile = recv_ref[step * FIRST_UNROLL + j]
        return tile, pltpu.roll(tile, 5, 0)

    pair_loop(ENTRIES // FIRST_UNROLL, FIRST_UNROLL, split_row(FIRST_UNROLL, row_ref), tile_of, near_ref, loc_ref, pot_ref, tail_ref, out_ref)


def contact_last(row_ref, home_ref, first_ref, x_ref, new_ref, disp_ref, vel_ref, loc_ref, near_ref, surf_ref):
    loc_ref[...] = jnp.zeros((ROWS, 8, NODES), f32)
    row = sublanes((8, NODES))
    for c in range(3):
        surf_ref[:, c, :] = disp_ref[c, DEPTH - 1]
        surf_ref[:, 3 + c, :] = vel_ref[c, DEPTH - 1]
        if c < 2:
            surf_ref[:, 6 + c, :] = jnp.zeros((ROWS, NODES), f32)
    consts = tile_constants()
    unit = unit_matrix()
    for b in range(ROWS):
        near_table(surf_ref[b], near_ref, b, unit, consts)

    def faced(e):
        vel = new_ref[e]
        return first_ref[e] + time_step * vel, vel

    def facing(e):
        tile = new_ref[e]
        vel = pltpu.roll(tile, 4, 0)
        x = pltpu.roll(wide_tile(x_ref[e]), 5, 0)
        y = pltpu.roll(tile, 6, 0)
        z = pltpu.roll(tile, 3, 0)
        disp = jnp.where(row == 0, x, jnp.where(row == 1, y, z))
        return disp + time_step * vel, vel

    faced_row = split_row(LAST_UNROLL, row_ref)

    def row_of(step, j):
        if j < LAST_UNROLL:
            return faced_row(step, j)
        return home_ref[step * LAST_UNROLL + j - LAST_UNROLL]

    def tile_of(step, j):
        if j < LAST_UNROLL:
            return faced(step * LAST_UNROLL + j)
        return facing(step * LAST_UNROLL + j - LAST_UNROLL)

    pair_loop(ENTRIES // LAST_UNROLL, 2 * LAST_UNROLL, row_of, tile_of, near_ref, loc_ref)


def plane_frame(c):
    if c != 1:
        return 0.0
    shape = (ROWS, NODES)
    return (lanes(shape).astype(f32) - (NODES - 1) / 2.0) * (frame_extent / NODES)


def plane_sum(loc_ref, disp, vel, c):
    weight = loc_ref[:, 3, :] + loc_ref[:, 7, :]
    potential = stiff_coef * (disp + plane_frame(c)) - damp_coef * vel
    return weight * potential - (loc_ref[:, c, :] + loc_ref[:, 4 + c, :])


def update_kernel(slot_ref, home_ref, row_ref, ret_ref, loc_ref, force_ref, disp_ref, vel_ref, mass_ref, *refs):
    new_disp, new_vel, send_hbm, send_ref, surf_ref, sum_ref, facing_tile, faced_tile, sems = refs

    def gather(b, carry):
        acc = ret_ref[slot_ref[b * FACES]]
        for k in range(1, FACES):
            acc = acc + ret_ref[slot_ref[b * FACES + k]]
        sum_ref[b] = acc
        return carry

    lax.fori_loop(0, ROWS, gather, 0, unroll=8)
    last = DEPTH - 1
    mass = time_step * mass_ref[last]
    for c in range(3):
        old, vel = disp_ref[c, last], vel_ref[c, last]
        vel = vel + mass * (force_ref[c, last] + sum_ref[:, c, :] + plane_sum(loc_ref, old, vel, c))
        new_vel[c, last] = vel
        new_disp[c, last] = old + time_step * vel
        surf_ref[:, c, :] = vel
        surf_ref[:, 3 + c, :] = old
    row = sublanes((8, NODES))

    def tiles(b, carry):
        tile = surf_ref[b]
        facing_tile[b] = jnp.where(row < 3, tile, 0.0)
        late = jnp.where(row < 7, pltpu.roll(tile, 4, 0), pltpu.roll(tile, 2, 0))
        faced_tile[b] = jnp.where(row < 3, 0.0, jnp.where(row == 3, pltpu.roll(tile, 7, 0), late))
        return carry

    lax.fori_loop(0, ROWS, tiles, 0, unroll=8)
    size = ENTRIES // CHUNKS
    copies = []
    for chunk in range(CHUNKS):

        def scatter(i, carry, chunk=chunk):
            for j in range(16):
                e = chunk * size + i * 16 + j
                at = (chunk * size) % NODES + i * 16 + j
                r = row_ref[chunk * size // NODES, at]
                send_ref[e] = facing_tile[home_ref[e]] + faced_tile[r]
            return carry

        lax.fori_loop(0, size // 16, scatter, 0)
        part = pl.ds(chunk * size, size)
        copies.append(pltpu.make_async_copy(send_ref.at[part], send_hbm.at[part], sems.at[chunk]))
        copies[-1].start()
    for z in range(DEPTH - 1):
        mass = time_step * mass_ref[z]
        for c in range(3):
            vel = vel_ref[c, z] + mass * force_ref[c, z]
            new_vel[c, z] = vel
            new_disp[c, z] = disp_ref[c, z] + time_step * vel
    for copy in copies:
        copy.wait()


def final_kernel(disp_ref, vel_ref, mass_ref, loc_ref, wide_in, node_in, row_lo, row_hi, col_lo, col_hi, *refs):
    new_disp, new_vel = refs

    def put(c, z, force):
        disp, vel = disp_ref[c, z], vel_ref[c, z]
        if z == DEPTH - 1:
            force = force + plane_sum(loc_ref, disp, vel, c)
        vel = vel + time_step * mass_ref[z] * force
        new_vel[c, z] = vel
        new_disp[c, z] = disp + time_step * vel

    force_kernel(False, disp_ref, wide_in, node_in, row_lo, row_hi, col_lo, col_hi, put)


VMEM = pl.BlockSpec(memory_space=pltpu.VMEM)
SMEM = pl.BlockSpec(memory_space=pltpu.SMEM)
HBM = pl.BlockSpec(memory_space=pltpu.HBM)


def struct(*shape, dtype=f32):
    return jax.ShapeDtypeStruct(shape, dtype)


def shifted(value, count_gx, count_gy, dx, dy):
    pairs = []
    for x in range(count_gx):
        for y in range(count_gy):
            if 0 <= x + dx < count_gx and 0 <= y + dy < count_gy:
                pairs.append((x * count_gy + y, (x + dx) * count_gy + y + dy))
    return lax.ppermute(value, AXES, pairs)


def scalars(value):
    return pltpu.with_memory_space_constraint(value, pltpu.SMEM)


def local(displacement, velocity, stiffness, inverse_mass, facing):
    count_gx = lax.axis_size("gx")
    count_gy = lax.axis_size("gy")
    disp = displacement.transpose(0, 2, 1, 3)
    vel = velocity.transpose(0, 2, 1, 3)
    stiff = stiffness.transpose(1, 0, 2)
    mass = inverse_mass.transpose(1, 0, 2)
    faces = facing.transpose(1, 2, 0).reshape(FACES, ROWS)
    ends = jnp.stack(
        [
            (lax.axis_index("gx") == count_gx - 1).astype(jnp.int32),
            (lax.axis_index("gy") == count_gy - 1).astype(jnp.int32),
        ]
    )
    send, slots, homes, surf = pl.pallas_call(
        request_kernel,
        in_specs=[HBM] * 3,
        out_specs=[VMEM, SMEM, SMEM, VMEM],
        out_shape=[
            struct(ENTRIES, 8, NODES),
            pltpu.SMEM((ENTRIES,), jnp.int32),
            pltpu.SMEM((ENTRIES,), jnp.int32),
            struct(ROWS, 8, NODES),
        ],
        scratch_shapes=[
            pltpu.SMEM((FACES, ROWS), jnp.int32),
            pltpu.VMEM((2, 3, ROWS, NODES), f32),
            pltpu.SMEM((NODES,), jnp.int32),
            pltpu.SemaphoreType.DMA((3,)),
        ],
        compiler_params=PARAMS,
        name="request",
    )(*(pltpu.with_memory_space_constraint(value, pltpu.HBM) for value in (faces, disp, vel)))
    near_shape = struct(ROWS, NODES, 48, dtype=bf16)
    tile_shape = struct(ROWS, 8, NODES)
    small_shape = struct(ROWS, 4, NODES)
    edge_shape = struct(ROWS, NODES)
    edge_shapes = [struct(24, NODES), struct(24, NODES), edge_shape, edge_shape]
    field_shape = struct(3, DEPTH, ROWS, NODES)
    entry_shape = struct(ENTRIES, 4, NODES)

    def go(value, dx, dy):
        return shifted(value, count_gx, count_gy, dx, dy)

    def exchange(value):
        return lax.all_to_all(value, AXES, 0, 0, tiled=True)

    def call(kernel, name, in_specs, out_specs, out_shape, scratch=()):
        return pl.pallas_call(
            kernel,
            in_specs=in_specs,
            out_specs=out_specs,
            out_shape=out_shape,
            scratch_shapes=scratch,
            compiler_params=PARAMS,
            name=name,
        )

    first = exchange(send)
    low_row, high_row, low_col, high_col, masked = call(
        lambda *refs: edge_kernel(True, *refs),
        "edges_first",
        [SMEM] + [VMEM] * 3,
        [VMEM] * 5,
        edge_shapes + [struct(DEPTH, ROWS, NODES)],
    )(ends, disp, surf, stiff)
    col_lo = go(high_col, 0, 1)
    col_hi = go(low_col, 0, -1)
    near, pot, tail = call(
        table_kernel,
        "tables_first",
        [VMEM],
        [VMEM] * 3,
        [near_shape, struct(ROWS, 16, NODES, dtype=bf16), small_shape],
    )(surf)
    action, reaction, low_out, high_out, rows = call(
        contact_first,
        "contact_first",
        [VMEM] * 8,
        [VMEM] * 4 + [SMEM],
        [entry_shape, tile_shape, edge_shape, edge_shape, pltpu.SMEM((ENTRIES // NODES, NODES), jnp.int32)],
        [pltpu.VMEM((ENTRIES // NODES, NODES), jnp.int32), pltpu.SemaphoreType.DMA(())],
    )(first, near, pot, tail, low_row, high_row, col_lo, col_hi)
    returned = exchange(action)
    row_lo = go(high_out, 1, 0)
    row_hi = go(low_out, -1, 0)
    force, wide, node = call(
        lambda *refs: force_kernel(True, *refs),
        "force_first",
        [VMEM] * 6,
        [VMEM] * 3,
        [field_shape, struct(DEPTH - 1, 2, ROWS + 8, NODES), struct(DEPTH, ROWS, NODES)],
    )(disp, masked, row_lo, row_hi, col_lo, col_hi)
    tiles = pltpu.VMEM((ROWS, 8, NODES), f32)
    disp, vel, send = call(
        update_kernel,
        "update_first",
        [SMEM] * 3 + [VMEM] * 6,
        [VMEM] * 2 + [HBM],
        [field_shape, field_shape, pltpu.HBM((ENTRIES, 8, NODES), f32)],
        [
            pltpu.VMEM((ENTRIES, 8, NODES), f32),
            tiles,
            pltpu.VMEM((ROWS, 4, NODES), f32),
            tiles,
            tiles,
            pltpu.SemaphoreType.DMA((CHUNKS,)),
        ],
    )(scalars(slots), scalars(homes), scalars(rows), returned, reaction, force, disp, vel, mass)

    news = exchange(send)
    low_row, high_row, low_col, high_col = call(
        lambda *refs: edge_kernel(False, *refs), "edges_last", [VMEM], [VMEM] * 4, edge_shapes
    )(disp)
    col_lo = go(high_col, 0, 1)
    col_hi = go(low_col, 0, -1)
    low_out, high_out = call(row_messages, "rows_last", [VMEM] * 4, [VMEM] * 2, [edge_shape] * 2)(
        low_row, high_row, col_lo, col_hi
    )
    row_lo = go(high_out, 1, 0)
    row_hi = go(low_out, -1, 0)
    (total,) = call(
        contact_last,
        "contact_last",
        [SMEM] * 2 + [VMEM] * 5,
        [VMEM],
        [tile_shape],
        [pltpu.VMEM((ROWS, NODES, 48), bf16), tiles],
    )(scalars(rows), scalars(homes), first, returned, news, disp, vel)
    disp, vel = call(final_kernel, "update_last", [VMEM] * 10, [VMEM] * 2, [field_shape] * 2)(
        disp, vel, mass, total, wide, node, row_lo, row_hi, col_lo, col_hi
    )
    return disp.transpose(0, 2, 1, 3), vel.transpose(0, 2, 1, 3)


def solution(mesh):
    in_specs = (
        P(None, "gx", None, "gy"),
        P(None, "gx", None, "gy"),
        P("gx", None, "gy"),
        P("gx", None, "gy"),
        P("gx", "gy", None),
    )
    out_specs = (P(None, "gx", None, "gy"), P(None, "gx", None, "gy"))
    return jax.shard_map(local, mesh=mesh, in_specs=in_specs, out_specs=out_specs, check_vma=False)
```
